256 devices in a mesh: pipe: 32 (over x_lo, z, core), ctx: 8 (over y, x_hi).
Axes of the slice: x: 4 (x_hi: 2, x_lo: 2; x = x_hi * 2 + x_lo), y: 4, z: 8, core: 2. Of those that a mesh axis runs over, the one named last changes fastest.
Arguments:
- inflow: bfloat16 [32, 2, 512, 3072], P('pipe', None, 'ctx'), may hold values from -6 to 6
- patches: bfloat16 [2, 512, 64], P(None, 'ctx'), may hold values from -6 to 6
- patch_weight: bfloat16 [64, 3072], replicated, may hold values from -0.75 to 0.75
- timesteps: int32 [2], replicated, may hold values from 0 to 999
- time_weight: bfloat16 [256, 3072], replicated, may hold values from -0.375 to 0.375
- mod_weight: bfloat16 [3072, 9216], P(('pipe', 'ctx')), may hold values from -0.109375 to 0.109375
- layer_table: bfloat16 [32, 9216], replicated, may hold values from -3 to 3
- section_layer: int32 [32], replicated, may hold values from 0 to 31, each once
- token_cell: int32 [512], replicated, may hold values from 0 to 511, each once
- q_weight: bfloat16 [32, 3072, 3072], P('pipe', None, 'ctx')
- k_weight: bfloat16 [32, 3072, 3072], P('pipe', None, 'ctx')
- v_weight: bfloat16 [32, 3072, 3072], P('pipe', None, 'ctx'), may hold values from -0.109375 to 0.109375
- out_weight: bfloat16 [32, 3072, 3072], P('pipe', 'ctx'), may hold values from -0.625 to 0.625
- q_gain: float32 [32, 3072], P('pipe', 'ctx'), may hold values from 0.6 to 5
- k_gain: float32 [32, 3072], P('pipe', 'ctx'), may hold values from 0.6 to 5
Outputs:
- handed_off: bfloat16 [32, 2, 512, 3072], P('pipe', None, 'ctx')
The draws below stay inside these ranges and needn't reach their ends.
Inputs may be any that keep to these rules, and one draw needn't show every extreme that they name: `section_layer`: each section runs a different layer. `token_cell`: each cell of the 512-token grid holds one token.
All inputs are finite; a program needn't handle non-finite values.
Results may differ from the reference program's by a relative error of at most 0.02.
Values may be sent and summed in bfloat16 or wider, within the bound.
A program may use at most 128 MiB of HBM per device.

```python
import jax
import jax.numpy as jnp
from jax import lax

D = 3072
HEADS = 24
HEAD = 128
PATCH = 64
FREQ = 256
MB = 2
GRID_H = 8
GRID_W = 16
A = 3072
TOKENS = 512
N_PIPE = 32


def column_scale(key, top_ratio):
    col_pos = jnp.arange(HEADS * HEAD, dtype=jnp.float32) / (HEADS * HEAD)
    rising = jnp.exp(jnp.log(top_ratio) * col_pos)[None, :]
    rough = jnp.exp(jax.random.uniform(jax.random.fold_in(key, 13), (N_PIPE, HEADS * HEAD), jnp.float32, jnp.log(0.7), jnp.log(1.4)))
    return rising * rough


def own_normal(own_key, scales):
    return jax.random.normal(own_key, (N_PIPE, D, HEADS * HEAD), jnp.float32) * D ** (-0.5) * scales


def draw_q_weight(key, part):
    own_key = jax.random.fold_in(key, 3)
    return own_normal(own_key, column_scale(key, 4.0)[:, None, :]).astype(jnp.bfloat16)


def draw_k_weight(key, part):
    own_key = jax.random.fold_in(key, 5)
    return own_normal(own_key, column_scale(key, 4.0)[:, None, :]).astype(jnp.bfloat16)


def gain_draw(key, own_key):
    shape_all = (N_PIPE, HEADS * HEAD)
    return jax.random.uniform(jax.random.fold_in(own_key, 1), shape_all, jnp.float32, 0.8, 1.25)


def draw_q_gain(key, part):
    own_key = jax.random.fold_in(key, 21)
    return gain_draw(key, own_key)


def draw_k_gain(key, part):
    own_key = jax.random.fold_in(key, 31)
    return gain_draw(key, own_key)


def block_scale(stream_key, extent, split, low, top_value):
    def one(position, parts):
        steps = jax.random.uniform(jax.random.fold_in(jax.random.fold_in(stream_key, 6), position), (parts,), jnp.float32, low / len(split), top_value / len(split))
        return jnp.repeat(jnp.exp(steps), extent[position] // parts).reshape((-1,) + (1,) * (len(extent) - position - 1))

    gain = one(*split[0])
    for cut in split[1:]:
        gain = gain * one(*cut)
    return gain


def noise(stream_key, extent, deviation, reach, pieces=(), kind=jnp.bfloat16):
    factor_of = block_scale(stream_key, extent, pieces, -0.22, 0.18) if pieces else 1.0
    result = jax.random.normal(stream_key, extent, jnp.float32) * deviation * factor_of
    return jnp.minimum(jnp.maximum(result, -reach), reach).astype(kind)


def setup_inputs(seed: int = 0) -> dict:
    splits = jax.random.split(jax.random.key(seed), 16)
    return {
        "inflow": noise(splits[0], (N_PIPE, MB, TOKENS, D), 1.0, 6.0, ((0, 32), (2, 8))),
        "patches": noise(splits[1], (MB, TOKENS, PATCH), 1.0, 6.0, ((1, 8),)),
        "patch_weight": noise(splits[2], (PATCH, D), PATCH ** -0.5, 0.75),
        "timesteps": jax.random.randint(splits[3], (MB,), 0, 1000).astype(jnp.int32),
        "time_weight": noise(splits[4], (FREQ, D), FREQ ** -0.5, 0.375),
        "mod_weight": noise(splits[5], (D, 3 * D), D ** -0.5, 0.109375, ((0, 256),)),
        "layer_table": noise(splits[6], (N_PIPE, 3 * D), 0.5, 3.0),
        "section_layer": jax.random.permutation(splits[7], N_PIPE).astype(jnp.int32),
        "token_cell": jax.random.permutation(splits[8], TOKENS).astype(jnp.int32),
        "q_weight": draw_q_weight(jax.random.fold_in(splits[15], 71), 0),
        "k_weight": draw_k_weight(jax.random.fold_in(splits[15], 71), 0),
        "v_weight": noise(splits[11], (N_PIPE, D, A), D ** -0.5, 0.109375, ((0, 32), (2, 8))),
        "out_weight": noise(splits[12], (N_PIPE, A, D), (A // 36) ** -0.5, 0.625, ((0, 32), (1, 8))),
        "q_gain": draw_q_gain(jax.random.fold_in(splits[15], 71), 0),
        "k_gain": draw_k_gain(jax.random.fold_in(splits[15], 71), 0),
    }


def time_features(timesteps):
    half_size = FREQ // 2
    rates = 10000.0 ** (-jnp.arange(half_size, dtype=jnp.float32) / half_size)
    angles = timesteps.astype(jnp.float32)[:, None] * rates[None, :]
    return jnp.concatenate([jnp.cos(angles), jnp.sin(angles)], 1).astype(jnp.bfloat16)

def rope_tables(token_cell):
    half_size = HEAD // 2
    time_pairs = half_size - 2 * (HEAD // 6)
    space_pairs = HEAD // 6
    frame_pos = token_cell // (GRID_H * GRID_W)
    row_pos = token_cell // GRID_W % GRID_H
    col_pos = token_cell % GRID_W
    pair_ids = jnp.arange(half_size, dtype=jnp.int32)
    positions = jnp.where(pair_ids[None, :] < time_pairs, frame_pos[:, None], jnp.where(pair_ids[None, :] < time_pairs + space_pairs, row_pos[:, None], col_pos[:, None]))
    pair_float = pair_ids.astype(jnp.float32)
    exponent = jnp.where(pair_ids < time_pairs, pair_float / time_pairs, jnp.where(pair_ids < time_pairs + space_pairs, (pair_float - time_pairs) / space_pairs, (pair_float - time_pairs - space_pairs) / space_pairs))
    angles = positions.astype(jnp.float32) * (10000.0 ** (-exponent))[None, :]
    return (jnp.cos(angles), jnp.sin(angles))

def rotate(heads_in, cos_table, sin_table):
    half_size = heads_in.shape[-1] // 2
    first_half = heads_in[..., :half_size]
    second_half = heads_in[..., half_size:]
    cos_b = cos_table[:, None, :]
    sin_b = sin_table[:, None, :]
    return jnp.concatenate([first_half * cos_b - second_half * sin_b, first_half * sin_b + second_half * cos_b], -1)

def block(stream, modulation, wq, wk, wv, wo, gq, gk, cos_table, sin_table):
    shift_mod = modulation[:D]
    scale_mod = modulation[D:2 * D]
    gate_mod = modulation[2 * D:]
    values_f = stream.astype(jnp.float32)
    center = values_f - lax.optimization_barrier(jnp.mean(values_f, -1, keepdims=True))
    spread = lax.optimization_barrier(jnp.mean(center * center, -1, keepdims=True))
    normed = (center * lax.rsqrt(spread + 1e-06) * (1.0 + scale_mod) + shift_mod).astype(jnp.bfloat16)
    q_raw = jnp.dot(normed, wq, preferred_element_type=jnp.float32)
    k_raw = jnp.dot(normed, wk, preferred_element_type=jnp.float32)
    val_all = jnp.dot(normed, wv, preferred_element_type=jnp.float32).astype(jnp.bfloat16)
    q_raw = q_raw * lax.rsqrt(lax.optimization_barrier(jnp.mean(q_raw * q_raw, -1, keepdims=True)) + 1e-06) * gq
    k_raw = k_raw * lax.rsqrt(lax.optimization_barrier(jnp.mean(k_raw * k_raw, -1, keepdims=True)) + 1e-06) * gk
    count = stream.shape[0]
    queries = rotate(q_raw.reshape(count, HEADS, HEAD), cos_table, sin_table).astype(jnp.bfloat16)
    keys_all = rotate(k_raw.reshape(count, HEADS, HEAD), cos_table, sin_table).astype(jnp.bfloat16)
    val_heads = val_all.reshape(count, HEADS, HEAD)
    scores = jnp.einsum('thd,shd->hts', queries.astype(jnp.float32), keys_all.astype(jnp.float32)) * HEAD ** (-0.5)
    scores = scores - lax.optimization_barrier(jnp.max(scores, -1, keepdims=True))
    weights = jnp.exp(scores)
    probs = (weights / lax.optimization_barrier(jnp.sum(weights, -1, keepdims=True))).astype(jnp.bfloat16)
    attended = jnp.einsum('hts,shd->thd', probs.astype(jnp.float32), val_heads.astype(jnp.float32)).astype(jnp.bfloat16)
    branch = jnp.dot(attended.reshape(count, HEADS * HEAD), wo, preferred_element_type=jnp.float32)
    return (values_f + gate_mod * branch).astype(jnp.bfloat16)

def reference(inflow, patches, patch_weight, timesteps, time_weight, mod_weight, layer_table, section_layer, token_cell, q_weight, k_weight, v_weight, out_weight, q_gain, k_gain):
    time_hidden = jax.nn.silu(jnp.dot(time_features(timesteps), time_weight, preferred_element_type=jnp.float32)).astype(jnp.bfloat16)
    mod_base = jnp.dot(time_hidden, mod_weight, preferred_element_type=jnp.float32)
    embedded = jnp.einsum('btp,pd->btd', patches.astype(jnp.float32), patch_weight.astype(jnp.float32)).astype(jnp.bfloat16)
    cos_table, sin_table = rope_tables(token_cell)

    def one_section(items):
        section, layer_id, wq, wk, wv, wo, gq, gk, stream_in = items
        modulation = mod_base + layer_table[layer_id].astype(jnp.float32)[None, :]
        start = jnp.where(section == 0, embedded, stream_in)
        outputs = [block(start[slot], modulation[slot], wq, wk, wv, wo, gq, gk, cos_table, sin_table) for slot in range(MB)]
        return jnp.stack(outputs)
    sections = jnp.arange(N_PIPE, dtype=jnp.int32)
    results = lax.map(one_section, (sections, section_layer, q_weight, k_weight, v_weight, out_weight, q_gain, k_gain, inflow))
    return jnp.concatenate([jnp.zeros_like(results[:1]), results[:-1]], 0)
```

```python
import functools

import jax
import jax.numpy as jnp
from jax import lax
from jax.experimental import pallas as pl
from jax.experimental.pallas import tpu as pltpu
from jax.sharding import PartitionSpec as P

HEAD = 128
GRID_H = 8
GRID_W = 16
MESH = pl.DeviceIdType.MESH
CTX = 8
CHUNK = 16

GATHER = 0
REDUCE = 8
STATS = 16
HAND = 23
PER_CLIP = 24


def time_features(timesteps, freq_count):
    half_size = freq_count // 2
    rates = 10000.0 ** (-jnp.arange(half_size, dtype=jnp.float32) / half_size)
    angles = timesteps.astype(jnp.float32)[:, None] * rates[None, :]
    return jnp.concatenate([jnp.cos(angles), jnp.sin(angles)], 1).astype(jnp.bfloat16)


def rope_tables(token_cell):
    half_size = HEAD // 2
    time_pairs = half_size - 2 * (HEAD // 6)
    space_pairs = HEAD // 6
    frame_pos = token_cell // (GRID_H * GRID_W)
    row_pos = token_cell // GRID_W % GRID_H
    col_pos = token_cell % GRID_W
    pair_ids = jnp.arange(half_size, dtype=jnp.int32)
    positions = jnp.where(
        pair_ids[None, :] < time_pairs,
        frame_pos[:, None],
        jnp.where(pair_ids[None, :] < time_pairs + space_pairs, row_pos[:, None], col_pos[:, None]),
    )
    pair_float = pair_ids.astype(jnp.float32)
    exponent = jnp.where(
        pair_ids < time_pairs,
        pair_float / time_pairs,
        jnp.where(
            pair_ids < time_pairs + space_pairs,
            (pair_float - time_pairs) / space_pairs,
            (pair_float - time_pairs - space_pairs) / space_pairs,
        ),
    )
    angles = positions.astype(jnp.float32) * (10000.0 ** (-exponent))[None, :]
    cos_half, sin_half = jnp.cos(angles), jnp.sin(angles)
    return jnp.concatenate([cos_half, cos_half], 1), jnp.concatenate([-sin_half, sin_half], 1)


def section_kernel(
    pipe_count,
    stream_in,
    mod_part,
    layer_row,
    cos_ref,
    sin_ref,
    q_weight,
    k_weight,
    v_weight,
    out_weight,
    q_gain,
    k_gain,
    out_ref,
    gathered,
    normed,
    w_all,
    w_out,
    raw,
    heads_q,
    heads_k,
    heads_v,
    attended,
    partial,
    got_full,
    got_half,
    stat_own,
    stat_got,
    columns,
    mod_sum,
    mod_got_a,
    mod_got_b,
    mod_got_c,
    mod_total,
    send_sems,
    recv_sems,
    mod_send,
    mod_recv,
    load_sems,
):
    clips, rows = stream_in.shape[0], stream_in.shape[1]
    width = stream_in.shape[2]
    local_cols = q_weight.shape[2]
    local_heads = local_cols // HEAD
    tokens = rows * CTX
    mod_cols = mod_part.shape[1] // CTX
    lanes_pipe = min(4, pipe_count)
    depth_pipe = pipe_count // lanes_pipe

    pipe = lax.axis_index("pipe")
    ctx = lax.axis_index("ctx")
    y, side = ctx // 2, ctx % 2

    def at_ctx(row, col):
        return lax.rem(row + 4, 4) * 2 + col

    c_up, c_down, c_far = at_ctx(y + 1, side), at_ctx(y - 1, side), at_ctx(y + 2, side)
    c_pair = at_ctx(y, 1 - side)
    c_pair_up, c_pair_down, c_pair_far = (
        at_ctx(y + 1, 1 - side),
        at_ctx(y - 1, 1 - side),
        at_ctx(y + 2, 1 - side),
    )
    up, down, pair = (pipe, c_up), (pipe, c_down), (pipe, c_pair)

    core = lax.rem(pipe, 2)
    if pipe_count >= 4:
        z = lax.rem(pipe // 2, depth_pipe)
        x_lo = pipe // (2 * depth_pipe)

        def depth_peer(step):
            return ((x_lo * depth_pipe + lax.rem(z + step, depth_pipe)) * 2 + core, ctx)

        def quad_peer(step):
            there = lax.rem(x_lo * 2 + core + step, 4)
            return (((there // 2) * depth_pipe + z) * 2 + lax.rem(there, 2), ctx)

    else:

        def depth_peer(step):
            return (pipe, ctx)

        def quad_peer(step):
            return (lax.rem(pipe + step, lanes_pipe), ctx)

    def ctx_peer(step):
        return (pipe, lax.rem(ctx + step, CTX))

    after = (lax.rem(pipe + 1, pipe_count), ctx)
    before = (lax.rem(pipe + pipe_count - 1, pipe_count), ctx)

    loads = [
        pltpu.make_async_copy(
            stream_in.at[m], gathered.at[m, pl.ds(pl.multiple_of(ctx * rows, rows), rows)], load_sems.at[m]
        )
        for m in range(clips)
    ]
    weights = [
        pltpu.make_async_copy(w.at[0], w_all.at[:, pl.ds(i * local_cols, local_cols)], load_sems.at[clips + i])
        for i, w in enumerate((q_weight, k_weight, v_weight))
    ] + [pltpu.make_async_copy(out_weight.at[0], w_out, load_sems.at[clips + 3])]
    for copy in loads:
        copy.start()

    greeted = (
        [ctx_peer(s) for s in range(1, CTX)]
        + [depth_peer(s) for s in range(1, depth_pipe)]
        + [quad_peer(s) for s in range(1, lanes_pipe)]
        + [after, before]
    )
    barrier = pltpu.get_barrier_semaphore()
    for peer in greeted:
        pl.semaphore_signal(barrier, inc=1, device_id=peer, device_id_type=MESH)
    pl.semaphore_wait(barrier, len(greeted))

    def remote(src, dst, number, peer, sends=send_sems, recvs=recv_sems):
        return pltpu.make_async_remote_copy(
            src_ref=src,
            dst_ref=dst,
            send_sem=sends.at[number],
            recv_sem=recvs.at[number],
            device_id=peer,
            device_id_type=MESH,
        )

    def block(ref, m, owner, first=0, count=rows):
        return ref.at[m, pl.ds(pl.multiple_of(owner * rows + first, 16), count)]

    half = rows // 2

    class Gather:
        def __init__(self, m):
            base = m * PER_CLIP + GATHER

            def send(owner, number, peer, first=0, count=rows):
                part = block(gathered, m, owner, first, count)
                return remote(part, part, base + number, peer)

            self.own = [send(ctx, 0, up), send(ctx, 1, down), send(ctx, 2, pair)]
            self.far_halves = [send(c_down, 3, up, 0, half), send(c_up, 4, down, half, half)]
            self.others = [send(c_pair, 5, up), send(c_pair, 6, down)]
            self.far_pair = [send(c_far, 7, pair)]
            self.all = self.own + self.far_halves + self.others + self.far_pair

        def start_own(self):
            for copy in self.own:
                copy.start()

        def forward_near(self):
            self.own[0].wait_recv()
            self.far_halves[0].start()
            self.own[1].wait_recv()
            self.far_halves[1].start()
            self.own[2].wait_recv()
            for copy in self.others:
                copy.start()

        def forward_far(self):
            for copy in self.far_halves:
                copy.wait_recv()
            self.far_pair[0].start()

        def finish(self):
            for copy in self.others + self.far_pair:
                copy.wait_recv()

        def drain(self):
            for copy in self.all:
                copy.wait_send()

    gathers = [Gather(m) for m in range(clips)]

    def add_into(m, owner, first, count, sources):
        def step(i, carry):
            at = pl.ds(pl.multiple_of(owner * rows + first + i * CHUNK, CHUNK), CHUNK)
            total = partial[m, at].astype(jnp.float32)
            for source in sources:
                total = total + source[pl.ds(i * CHUNK, CHUNK)].astype(jnp.float32)
            partial[m, at] = total.astype(jnp.bfloat16)
            return carry

        lax.fori_loop(0, count // CHUNK, step, 0)

    class Reduce:
        def __init__(self, m):
            self.m = m
            base = m * PER_CLIP + REDUCE
            full = [got_full.at[m, i] for i in range(6)]
            halves = [got_half.at[m, i] for i in range(2)]
            self.full, self.halves = full, halves

            def send(owner, number, peer, into, first=0, count=rows):
                return remote(block(partial, m, owner, first, count), into, base + number, peer)

            self.far_pair = send(c_pair_far, 0, pair, full[0])
            self.other_up = send(c_pair_up, 1, up, full[1])
            self.other_down = send(c_pair_down, 2, down, full[2])
            self.far_down = send(c_far, 3, down, halves[0], 0, half)
            self.far_up = send(c_far, 4, up, halves[1], half, half)
            self.near_down = send(c_down, 5, down, full[3])
            self.near_up = send(c_up, 6, up, full[4])
            self.pair = send(c_pair, 7, pair, full[5])
            self.all = [
                self.far_pair,
                self.other_up,
                self.other_down,
                self.far_down,
                self.far_up,
                self.near_down,
                self.near_up,
                self.pair,
            ]

        def start(self):
            self.far_pair.start()
            self.other_up.start()
            self.other_down.start()

        def second(self):
            self.far_pair.wait_recv()
            add_into(self.m, c_far, 0, rows, [self.full[0]])
            self.far_down.start()
            self.far_up.start()
            self.other_up.wait_recv()
            self.other_down.wait_recv()
            add_into(self.m, c_pair, 0, rows, [self.full[1], self.full[2]])
            self.pair.start()

        def third(self):
            self.far_down.wait_recv()
            add_into(self.m, c_down, 0, half, [self.halves[0]])
            self.near_down.start()
            self.far_up.wait_recv()
            add_into(self.m, c_up, half, half, [self.halves[1]])
            self.near_up.start()

        def last(self):
            self.near_down.wait_recv()
            self.near_up.wait_recv()
            self.pair.wait_recv()
            m = self.m
            gate = mod_total[pl.ds(m, 1), 2 * width : 3 * width] + layer_row[:, 2 * width : 3 * width]

            def step(i, carry):
                at = pl.ds(pl.multiple_of(ctx * rows + i * CHUNK, CHUNK), CHUNK)
                here = pl.ds(i * CHUNK, CHUNK)
                branch = partial[m, at].astype(jnp.float32)
                for source in self.full[3:]:
                    branch = branch + source[here].astype(jnp.float32)
                result = gathered[m, at].astype(jnp.float32) + gate * branch
                partial[m, at] = result.astype(jnp.bfloat16)
                return carry

            lax.fori_loop(0, rows // CHUNK, step, 0)

        def drain(self):
            for copy in self.all:
                copy.wait_send()

    reduces = [Reduce(m) for m in range(clips)]
    hands = [
        remote(block(partial, m, ctx), out_ref.at[m], m * PER_CLIP + HAND, after) for m in range(clips)
    ]

    def hand_off(m):
        @pl.when(pipe < pipe_count - 1)
        def _():
            hands[m].start()

    def norm_block(m, owner):
        shift = mod_total[pl.ds(m, 1), 0:width] + layer_row[:, 0:width]
        scale = 1.0 + (mod_total[pl.ds(m, 1), width : 2 * width] + layer_row[:, width : 2 * width])

        def step(i, carry):
            at = pl.ds(pl.multiple_of(owner * rows + i * CHUNK, CHUNK), CHUNK)
            values = gathered[m, at].astype(jnp.float32)
            center = values - jnp.mean(values, -1, keepdims=True)
            spread = jnp.mean(center * center, -1, keepdims=True)
            normed[m, at] = (center * lax.rsqrt(spread + 1e-06) * scale + shift).astype(jnp.bfloat16)
            return carry

        lax.fori_loop(0, rows // CHUNK, step, 0)

    def project(m):
        def step(i, carry):
            cols = pl.ds(pl.multiple_of(i * local_cols, local_cols), local_cols)
            raw[:, cols] = jnp.dot(normed[m], w_all[:, cols], preferred_element_type=jnp.float32)
            return carry

        lax.fori_loop(0, 3, step, 0)

    stat_sends = [
        [
            remote(stat_own.at[m], stat_got.at[m, s - 1], m * PER_CLIP + STATS + s - 1, ctx_peer(s))
            for s in range(1, CTX)
        ]
        for m in range(clips)
    ]

    def start_stats(m):
        q_raw = raw[:, 0:local_cols]
        k_raw = raw[:, local_cols : 2 * local_cols]
        q_sum = jnp.sum(q_raw * q_raw, -1, keepdims=True)
        k_sum = jnp.sum(k_raw * k_raw, -1, keepdims=True)
        lane = lax.broadcasted_iota(jnp.int32, (tokens, HEAD), 1)
        both = jnp.where(lane == 0, q_sum, k_sum)
        stat_own[m] = both.T[0:2]
        for copy in stat_sends[m]:
            copy.start()

    def finish_stats(m):
        total = stat_own[m]
        for s, copy in enumerate(stat_sends[m]):
            copy.wait_recv()
            total = total + stat_got[m, s]
        inverse = lax.rsqrt(total / width + 1e-06)
        columns[...] = jnp.concatenate([inverse, jnp.zeros((HEAD - 2, tokens), jnp.float32)], 0).T

    def rope(m):
        def step(h, carry):
            for kind, (gain, target) in enumerate(((q_gain, heads_q), (k_gain, heads_k))):
                here = pl.ds(pl.multiple_of(h * HEAD, HEAD), HEAD)
                there = pl.ds(pl.multiple_of(kind * local_cols + h * HEAD, HEAD), HEAD)
                value = raw[:, there] * columns[:, kind : kind + 1] * gain[:, here]
                turned = value * cos_ref[...] + pltpu.roll(value, HEAD // 2, 1) * sin_ref[...]
                target[:, here] = turned.astype(jnp.bfloat16)
            return carry

        lax.fori_loop(0, local_heads, step, 0)
        heads_v[...] = raw[:, 2 * local_cols : 3 * local_cols].astype(jnp.bfloat16)

    q_rows = 256

    def attend(m):
        def step(i, carry):
            h, r = i // (tokens // q_rows), lax.rem(i, tokens // q_rows)
            here = pl.ds(pl.multiple_of(h * HEAD, HEAD), HEAD)
            at = pl.ds(pl.multiple_of(r * q_rows, q_rows), q_rows)
            scores = lax.dot_general(
                heads_q[at, here], heads_k[:, here], (((1,), (1,)), ((), ())), preferred_element_type=jnp.float32
            ) * HEAD ** (-0.5)
            scores = scores - jnp.max(scores, -1, keepdims=True)
            weights = jnp.exp(scores)
            total = jnp.sum(weights, -1, keepdims=True)
            mixed = jnp.dot(weights.astype(jnp.bfloat16), heads_v[:, here], preferred_element_type=jnp.float32)
            attended[at, here] = (mixed / total).astype(jnp.bfloat16)
            return carry

        lax.fori_loop(0, local_heads * (tokens // q_rows), step, 0)

    out_cols = 512

    def project_out(m):
        def step(i, carry):
            cols = pl.ds(pl.multiple_of(i * out_cols, out_cols), out_cols)
            partial[m, :, cols] = jnp.dot(
                attended[...], w_out[:, cols], preferred_element_type=jnp.float32
            ).astype(jnp.bfloat16)
            return carry

        lax.fori_loop(0, width // out_cols, step, 0)

    def mod_slice(ref, index):
        return ref.at[:, pl.ds(pl.multiple_of(index * mod_cols, 128), mod_cols)]

    mod_a = [
        remote(
            mod_slice(mod_part, lax.rem(ctx + s, CTX)), mod_got_a.at[s - 1], s - 1, ctx_peer(s), mod_send, mod_recv
        )
        for s in range(1, CTX)
    ]
    number = CTX - 1
    mod_b = [
        remote(mod_sum.at[0], mod_got_b.at[s - 1], number + s - 1, depth_peer(s), mod_send, mod_recv)
        for s in range(1, depth_pipe)
    ]
    number += depth_pipe - 1
    mod_c = [
        remote(mod_sum.at[1], mod_got_c.at[s - 1], number + s - 1, quad_peer(s), mod_send, mod_recv)
        for s in range(1, lanes_pipe)
    ]
    number += lanes_pipe - 1
    mod_d = [
        remote(mod_slice(mod_total, ctx), mod_slice(mod_total, ctx), number + s - 1, ctx_peer(s), mod_send, mod_recv)
        for s in range(1, CTX)
    ]
    own_cols = pl.ds(pl.multiple_of(ctx * mod_cols, 128), mod_cols)

    def summed(value, copies, got):
        for i, copy in enumerate(copies):
            copy.wait_recv()
            value = value + got[i]
        return value

    for copy in mod_a:
        copy.start()
    for copy in loads:
        copy.wait()
    gathers[0].start_own()
    for copy in weights:
        copy.start()
    mod_sum[0] = summed(mod_part[:, own_cols], mod_a, mod_got_a)
    for copy in mod_b:
        copy.start()
    mod_sum[1] = summed(mod_sum[0], mod_b, mod_got_b)
    for copy in mod_c:
        copy.start()
    mod_total[:, own_cols] = summed(mod_sum[1], mod_c, mod_got_c)
    for copy in mod_d:
        copy.start()
    gathers[0].forward_near()
    for copy in mod_d:
        copy.wait_recv()
    for owner in (ctx, c_up, c_down, c_pair):
        norm_block(0, owner)
    gathers[0].forward_far()
    gathers[1].start_own()
    norm_block(0, c_far)
    for copy in weights:
        copy.wait()
    gathers[0].finish()
    for owner in (c_pair_up, c_pair_down, c_pair_far):
        norm_block(0, owner)
    project(0)
    start_stats(0)
    gathers[1].forward_near()
    for owner in (ctx, c_up, c_down, c_pair):
        norm_block(1, owner)
    finish_stats(0)
    rope(0)
    gathers[1].forward_far()
    attend(0)
    project_out(0)
    reduces[0].start()
    norm_block(1, c_far)
    gathers[1].finish()
    for owner in (c_pair_up, c_pair_down, c_pair_far):
        norm_block(1, owner)
    project(1)
    start_stats(1)
    reduces[0].second()
    finish_stats(1)
    rope(1)
    reduces[0].third()
    attend(1)
    project_out(1)
    reduces[1].start()
    reduces[0].last()
    hand_off(0)
    reduces[1].second()
    reduces[1].third()
    reduces[1].last()
    hand_off(1)

    for gather in gathers:
        gather.drain()
    for reduce in reduces:
        reduce.drain()
    for copy in mod_a + mod_b + mod_c + mod_d:
        copy.wait_send()
    for sends in stat_sends:
        for copy in sends:
            copy.wait_send()

    @pl.when(pipe < pipe_count - 1)
    def _():
        for copy in hands:
            copy.wait_send()

    @pl.when(pipe > 0)
    def _():
        for copy in hands:
            copy.wait_recv()

    @pl.when(pipe == 0)
    def _():
        out_ref[...] = jnp.zeros_like(out_ref)


def shards(
    inflow,
    patches,
    patch_weight,
    timesteps,
    time_weight,
    mod_weight,
    layer_table,
    section_layer,
    token_cell,
    q_weight,
    k_weight,
    v_weight,
    out_weight,
    q_gain,
    k_gain,
):
    clips, rows, width = inflow.shape[1:]
    local_cols = q_weight.shape[2]
    tokens = rows * CTX
    pipe_count = lax.axis_size("pipe")
    section = lax.axis_index("pipe")
    time_hidden = jax.nn.silu(
        jnp.dot(
            time_features(timesteps, time_weight.shape[0]),
            time_weight,
            preferred_element_type=jnp.float32,
        )
    ).astype(jnp.bfloat16)
    share_rows = mod_weight.shape[0]
    flat_rank = lax.axis_index(("pipe", "ctx"))
    time_piece = lax.dynamic_slice_in_dim(time_hidden, flat_rank * share_rows, share_rows, 1)
    mod_part = jnp.dot(time_piece, mod_weight, preferred_element_type=jnp.float32)
    section_ids = jnp.arange(section_layer.shape[0], dtype=jnp.int32)
    layer_id = jnp.sum(jnp.where(section_ids == section, section_layer, 0))
    layer_row = jnp.sum(
        jnp.where((section_ids == layer_id)[:, None], layer_table.astype(jnp.float32), 0.0), 0, keepdims=True
    )
    embedded = jnp.einsum(
        "btp,pd->btd", patches, patch_weight, preferred_element_type=jnp.float32
    ).astype(jnp.bfloat16)
    start_block = jnp.where(section == 0, embedded, inflow[0])
    cos_table, sin_table = rope_tables(token_cell)

    vmem = pl.BlockSpec(memory_space=pltpu.VMEM)
    anywhere = pl.BlockSpec(memory_space=pl.ANY)
    mod_width = layer_row.shape[1]
    mod_cols = mod_width // CTX
    lanes_pipe = min(4, pipe_count)
    depth_pipe = pipe_count // lanes_pipe
    mod_copies = 2 * (CTX - 1) + depth_pipe - 1 + lanes_pipe - 1
    bf16, f32 = jnp.bfloat16, jnp.float32
    handed = pl.pallas_call(
        functools.partial(section_kernel, pipe_count),
        out_shape=jax.ShapeDtypeStruct((clips, rows, width), bf16),
        in_specs=[anywhere, vmem, vmem, vmem, vmem, anywhere, anywhere, anywhere, anywhere, vmem, vmem],
        out_specs=vmem,
        scratch_shapes=[
            pltpu.VMEM((clips, tokens, width), bf16),
            pltpu.VMEM((clips, tokens, width), bf16),
            pltpu.VMEM((width, 3 * local_cols), bf16),
            pltpu.VMEM((local_cols, width), bf16),
            pltpu.VMEM((tokens, 3 * local_cols), f32),
            pltpu.VMEM((tokens, local_cols), bf16),
            pltpu.VMEM((tokens, local_cols), bf16),
            pltpu.VMEM((tokens, local_cols), bf16),
            pltpu.VMEM((tokens, local_cols), bf16),
            pltpu.VMEM((clips, tokens, width), bf16),
            pltpu.VMEM((clips, 6, rows, width), bf16),
            pltpu.VMEM((clips, 2, rows // 2, width), bf16),
            pltpu.VMEM((clips, 2, tokens), f32),
            pltpu.VMEM((clips, CTX - 1, 2, tokens), f32),
            pltpu.VMEM((tokens, HEAD), f32),
            pltpu.VMEM((2, clips, mod_cols), f32),
            pltpu.VMEM((CTX - 1, clips, mod_cols), f32),
            pltpu.VMEM((max(depth_pipe - 1, 1), clips, mod_cols), f32),
            pltpu.VMEM((max(lanes_pipe - 1, 1), clips, mod_cols), f32),
            pltpu.VMEM((clips, mod_width), f32),
            pltpu.SemaphoreType.DMA((clips * PER_CLIP,)),
            pltpu.SemaphoreType.DMA((clips * PER_CLIP,)),
            pltpu.SemaphoreType.DMA((mod_copies,)),
            pltpu.SemaphoreType.DMA((mod_copies,)),
            pltpu.SemaphoreType.DMA((clips + 4,)),
        ],
        compiler_params=pltpu.CompilerParams(
            collective_id=0, has_side_effects=True, vmem_limit_bytes=56 * 2**20
        ),
        cost_estimate=pl.CostEstimate(
            flops=2 * clips * tokens * width * local_cols * 4, bytes_accessed=4 * width * local_cols * 2, transcendentals=0
        ),
    )(
        start_block,
        mod_part,
        layer_row,
        cos_table,
        sin_table,
        q_weight,
        k_weight,
        v_weight,
        out_weight,
        q_gain,
        k_gain,
    )
    return handed[None]


def solution(mesh):
    placed = (
        P("pipe", None, "ctx", None),
        P(None, "ctx", None),
        P(),
        P(),
        P(),
        P(("pipe", "ctx"), None),
        P(),
        P(),
        P(),
        P("pipe", None, "ctx"),
        P("pipe", None, "ctx"),
        P("pipe", None, "ctx"),
        P("pipe", "ctx", None),
        P("pipe", "ctx"),
        P("pipe", "ctx"),
    )
    return jax.shard_map(
        shards, mesh=mesh, in_specs=placed, out_specs=P("pipe", None, "ctx", None), check_vma=False
    )
```

```python
import functools

import jax
import jax.numpy as jnp
import numpy as np
from jax import lax
from jax.experimental import pallas as pl
from jax.experimental.pallas import tpu as pltpu
from jax.sharding import PartitionSpec as P

HEAD = 128
GRID_H = 8
GRID_W = 16
MESH = pl.DeviceIdType.MESH
CTX = 8
CHUNK = 16
SPACE_PAIRS = HEAD // 6
TIME_PAIRS = HEAD // 2 - 2 * SPACE_PAIRS

GATHER_PARTS = (2, 2)
REDUCE_PARTS = (2, 3)
PARTS = 3
GATHER = 0
REDUCE = 10
PER_PART = 21
STATS = CTX - 1


def column_parts(width, parts):
    span = width // parts
    cross = span // 6 // 128 * 128
    return [
        (slice(p * span, (p + 1) * span), slice(p * span, (p + 1) * span - cross), slice((p + 1) * span - cross, (p + 1) * span))
        for p in range(parts)
    ]


def rate_rows(freq_count):
    half_freq = freq_count // 2
    time_rates = 10000.0 ** (-np.arange(half_freq) / half_freq)
    half_size = HEAD // 2
    pair_ids = np.arange(half_size)
    exponent = np.where(
        pair_ids < TIME_PAIRS,
        pair_ids / TIME_PAIRS,
        np.where(
            pair_ids < TIME_PAIRS + SPACE_PAIRS,
            (pair_ids - TIME_PAIRS) / SPACE_PAIRS,
            (pair_ids - TIME_PAIRS - SPACE_PAIRS) / SPACE_PAIRS,
        ),
    )
    table = np.zeros((8, max(freq_count, HEAD)), np.float32)
    table[0, :freq_count] = np.concatenate([time_rates, time_rates])
    table[1, :HEAD] = np.concatenate([10000.0 ** (-exponent)] * 2)
    return table


def section_kernel(
    pipe_count,
    timesteps,
    section_layer,
    inflow,
    patches,
    patch_weight,
    time_weight,
    mod_weight,
    layer_table,
    token_cell,
    rates,
    q_weight,
    k_weight,
    v_weight,
    out_weight,
    q_gain,
    k_gain,
    out_ref,
    gathered,
    normed,
    w_all,
    w_out,
    raw,
    heads_q,
    heads_k,
    heads_v,
    attended,
    partial,
    got_full,
    got_half,
    got_cross,
    stat_own,
    stat_got,
    columns,
    mod_sum,
    mod_got_a,
    mod_got_b,
    mod_got_c,
    mod_total,
    mod_part,
    modulation,
    cos_ref,
    sin_ref,
    w_time,
    w_patch,
    w_layer,
    patch_rows,
    send_sems,
    recv_sems,
    mod_send,
    mod_recv,
    load_sems,
):
    clips, rows, width = inflow.shape[1:]
    local_cols = q_weight.shape[2]
    local_heads = local_cols // HEAD
    tokens = rows * CTX
    mod_cols = mod_part.shape[1] // CTX
    lanes_pipe = min(4, pipe_count)
    depth_pipe = pipe_count // lanes_pipe

    pipe = lax.axis_index("pipe")
    ctx = lax.axis_index("ctx")
    y, side = ctx // 2, ctx % 2

    def at_ctx(row, col):
        return lax.rem(row + 4, 4) * 2 + col

    c_up, c_down, c_far = at_ctx(y + 1, side), at_ctx(y - 1, side), at_ctx(y + 2, side)
    c_pair = at_ctx(y, 1 - side)
    c_pair_up, c_pair_down, c_pair_far = (
        at_ctx(y + 1, 1 - side),
        at_ctx(y - 1, 1 - side),
        at_ctx(y + 2, 1 - side),
    )
    up, down, pair = (pipe, c_up), (pipe, c_down), (pipe, c_pair)

    core = lax.rem(pipe, 2)
    if pipe_count >= 4:
        z = lax.rem(pipe // 2, depth_pipe)
        x_lo = pipe // (2 * depth_pipe)

        def depth_peer(step):
            return ((x_lo * depth_pipe + lax.rem(z + step, depth_pipe)) * 2 + core, ctx)

        def quad_peer(step):
            there = lax.rem(x_lo * 2 + core + step, 4)
            return (((there // 2) * depth_pipe + z) * 2 + lax.rem(there, 2), ctx)

    else:

        def depth_peer(step):
            return (pipe, ctx)

        def quad_peer(step):
            return (lax.rem(pipe + step, lanes_pipe), ctx)

    def ctx_peer(step):
        return (pipe, lax.rem(ctx + step, CTX))

    after = (lax.rem(pipe + 1, pipe_count), ctx)
    before = (lax.rem(pipe + pipe_count - 1, pipe_count), ctx)

    def own_rows(m):
        return gathered.at[m, pl.ds(pl.multiple_of(ctx * rows, rows), rows)]

    loads = [pltpu.make_async_copy(inflow.at[0, m], own_rows(m), load_sems.at[m]) for m in range(clips)]
    share = mod_weight.shape[0]
    time_cols = w_time.shape[1]
    shares = time_cols // share
    rank = pipe * CTX + ctx
    time_load = pltpu.make_async_copy(
        time_weight.at[:, pl.ds(pl.multiple_of((rank // shares) * time_cols, 128), time_cols)],
        w_time,
        load_sems.at[clips],
    )
    layer_load = pltpu.make_async_copy(layer_table, w_layer, load_sems.at[clips + 1])
    patch_loads = [
        pltpu.make_async_copy(patch_weight, w_patch, load_sems.at[clips + 2]),
        pltpu.make_async_copy(patches, patch_rows, load_sems.at[clips + 3]),
    ]
    weights = [
        pltpu.make_async_copy(w.at[0], w_all.at[:, pl.ds(i * local_cols, local_cols)], load_sems.at[clips + 4 + i])
        for i, w in enumerate((q_weight, k_weight, v_weight))
    ] + [pltpu.make_async_copy(out_weight.at[0], w_out, load_sems.at[clips + 7])]

    @pl.when(pipe > 0)
    def _():
        for copy in loads:
            copy.start()

    @pl.when(pipe == 0)
    def _():
        for copy in patch_loads:
            copy.start()

    time_load.start()
    layer_load.start()

    greeted = (
        [ctx_peer(s) for s in range(1, CTX)]
        + [depth_peer(s) for s in range(1, depth_pipe)]
        + [quad_peer(s) for s in range(1, lanes_pipe)]
        + [after, before]
    )
    barrier = pltpu.get_barrier_semaphore()
    for peer in greeted:
        pl.semaphore_signal(barrier, inc=1, device_id=peer, device_id_type=MESH)

    lane = lax.broadcasted_iota(jnp.int32, (8, rates.shape[1]), 1)
    line = lax.broadcasted_iota(jnp.int32, (8, rates.shape[1]), 0)
    steps = jnp.where(line == 0, timesteps[0], timesteps[1]).astype(jnp.float32)
    angles = steps * rates[0:1, :]
    features = jnp.where(lane < rates.shape[1] // 2, jnp.cos(angles), jnp.sin(angles)).astype(jnp.bfloat16)
    time_load.wait()
    time_hidden = jax.nn.silu(
        jnp.dot(features, w_time[...], preferred_element_type=jnp.float32)
    ).astype(jnp.bfloat16)
    first = lax.rem(rank, shares) * share
    picked = lax.broadcasted_iota(jnp.int32, (time_cols, 128), 0) - first
    picks = (picked == lax.broadcasted_iota(jnp.int32, (time_cols, 128), 1)).astype(jnp.bfloat16)
    time_piece = jnp.dot(time_hidden, picks, preferred_element_type=jnp.float32).astype(jnp.bfloat16)
    mod_part[...] = jnp.dot(
        time_piece[:, :share], mod_weight[...], preferred_element_type=jnp.float32
    )[:clips]

    @pl.when(pipe == 0)
    def _():
        for copy in patch_loads:
            copy.wait()
        for m in range(clips):
            embedded = jnp.dot(patch_rows[m], w_patch[...], preferred_element_type=jnp.float32)
            gathered[m, pl.ds(pl.multiple_of(ctx * rows, rows), rows)] = embedded.astype(jnp.bfloat16)

    @pl.when(pipe > 0)
    def _():
        for copy in loads:
            copy.wait()

    pl.semaphore_wait(barrier, len(greeted))

    def remote(src, dst, number, peer, sends=send_sems, recvs=recv_sems):
        return pltpu.make_async_remote_copy(
            src_ref=src,
            dst_ref=dst,
            send_sem=sends.at[number],
            recv_sem=recvs.at[number],
            device_id=peer,
            device_id_type=MESH,
        )

    def block(ref, m, owner, first=0, count=rows, cols=slice(None)):
        return ref.at[m, pl.ds(pl.multiple_of(owner * rows + first, 16), count), cols]

    half = rows // 2

    class Gather:
        def __init__(self, m, part, columns_of):
            base = (m * PARTS + part) * PER_PART + GATHER
            whole, straight, crossing = columns_of

            def send(owner, number, peer, first=0, count=rows, cols=whole):
                piece = block(gathered if m == 0 else normed, m, owner, first, count, cols)
                return remote(piece, piece, base + number, peer)

            self.own = [send(ctx, 0, up), send(ctx, 1, down), send(ctx, 2, pair)]
            self.far_up = send(c_down, 3, up, 0, half)
            self.far_down = send(c_up, 4, down, half, half)
            self.other_up = send(c_pair, 5, up, cols=straight)
            self.other_down = send(c_pair, 6, down, cols=straight)
            self.far_pair = send(c_far, 7, pair)
            self.cross_up = send(c_down, 8, pair, cols=crossing)
            self.cross_down = send(c_up, 9, pair, cols=crossing)
            self.rest = [self.other_up, self.other_down, self.cross_up, self.cross_down, self.far_pair]
            self.all = self.own + [self.far_up, self.far_down] + self.rest

        def start(self):
            for copy in self.own:
                copy.start()

        def near_up(self):
            self.own[0].wait_recv()
            self.far_up.start()
            self.cross_up.start()

        def near_down(self):
            self.own[1].wait_recv()
            self.far_down.start()
            self.cross_down.start()

        def near_pair(self):
            self.own[2].wait_recv()
            self.other_up.start()
            self.other_down.start()

        def far(self):
            self.far_up.wait_recv()
            self.far_down.wait_recv()
            self.far_pair.start()

        def finish(self):
            for copy in self.rest:
                copy.wait_recv()

        def drain(self):
            for copy in self.all:
                copy.wait_send()

    gathers = [
        [Gather(m, i, columns_of) for i, columns_of in enumerate(column_parts(width, parts))]
        for m, parts in enumerate(GATHER_PARTS)
    ]

    def add_into(m, owner, first, count, sources, cols):
        def step(i, carry):
            at = pl.ds(pl.multiple_of(owner * rows + first + i * CHUNK, CHUNK), CHUNK)
            total = partial[m, at, cols].astype(jnp.float32)
            for source in sources:
                total = total + source[pl.ds(i * CHUNK, CHUNK), cols].astype(jnp.float32)
            partial[m, at, cols] = total.astype(jnp.bfloat16)
            return carry

        lax.fori_loop(0, count // CHUNK, step, 0)

    class Reduce:
        def __init__(self, m, part, columns_of):
            self.m = m
            base = (m * PARTS + part) * PER_PART + REDUCE
            self.whole, self.straight, self.crossing = whole, straight, crossing = columns_of

            def send(owner, number, peer, into, first=0, count=rows, cols=whole):
                return remote(
                    block(partial, m, owner, first, count, cols), into.at[:, cols], base + number, peer
                )

            self.full = full = [got_full.at[m, i] for i in range(6)]
            self.halves = halves = [got_half.at[m, i] for i in range(2)]
            self.crossed = crossed = [got_cross.at[m, i] for i in range(2)]
            self.far_pair = send(c_pair_far, 0, pair, full[0])
            self.other_up = send(c_pair_up, 1, up, full[1], cols=straight)
            self.other_down = send(c_pair_down, 2, down, full[2], cols=straight)
            self.cross_up = send(c_pair_up, 8, pair, crossed[0], cols=crossing)
            self.cross_down = send(c_pair_down, 9, pair, crossed[1], cols=crossing)
            self.hand = remote(block(partial, m, ctx, cols=whole), out_ref.at[m, :, whole], base + 10, after)
            self.far_down = send(c_far, 3, down, halves[0], 0, half)
            self.far_up = send(c_far, 4, up, halves[1], half, half)
            self.near_down = send(c_down, 5, down, full[3])
            self.near_up = send(c_up, 6, up, full[4])
            self.pair = send(c_pair, 7, pair, full[5])
            self.all = [
                self.far_pair,
                self.other_up,
                self.other_down,
                self.far_down,
                self.far_up,
                self.near_down,
                self.near_up,
                self.pair,
                self.cross_up,
                self.cross_down,
            ]

        def start(self):
            self.far_pair.start()
            self.other_up.start()
            self.other_down.start()
            self.cross_up.start()
            self.cross_down.start()

        def add_far(self):
            self.far_pair.wait_recv()
            add_into(self.m, c_far, 0, rows, [self.full[0]], self.whole)
            self.far_down.start()
            self.far_up.start()

        def add_pair(self):
            self.other_up.wait_recv()
            self.other_down.wait_recv()
            add_into(self.m, c_pair, 0, rows, self.full[1:3], self.straight)
            self.pair.start()

        def add_cross(self):
            self.cross_up.wait_recv()
            self.cross_down.wait_recv()
            add_into(self.m, c_up, 0, rows, [self.crossed[0]], self.crossing)
            add_into(self.m, c_down, 0, rows, [self.crossed[1]], self.crossing)

        def add_near(self):
            self.far_down.wait_recv()
            add_into(self.m, c_down, 0, half, [self.halves[0]], self.whole)
            self.near_down.start()
            self.far_up.wait_recv()
            add_into(self.m, c_up, half, half, [self.halves[1]], self.whole)
            self.near_up.start()

        def last(self):
            self.near_down.wait_recv()
            self.near_up.wait_recv()
            self.pair.wait_recv()
            m = self.m
            cols = self.whole
            gate = modulation[pl.ds(m, 1), 2 * width + cols.start : 2 * width + cols.stop]

            def step(i, carry):
                at = pl.ds(pl.multiple_of(ctx * rows + i * CHUNK, CHUNK), CHUNK)
                here = pl.ds(i * CHUNK, CHUNK)
                branch = partial[m, at, cols].astype(jnp.float32)
                for source in self.full[3:]:
                    branch = branch + source[here, cols].astype(jnp.float32)
                result = gathered[m, at, cols].astype(jnp.float32) + gate * branch
                partial[m, at, cols] = result.astype(jnp.bfloat16)
                return carry

            lax.fori_loop(0, rows // CHUNK, step, 0)

            @pl.when(pipe < pipe_count - 1)
            def _():
                self.hand.start()

        def drain(self):
            for copy in self.all:
                copy.wait_send()

    reduces = [
        [Reduce(m, i, columns_of) for i, columns_of in enumerate(column_parts(width, parts))]
        for m, parts in enumerate(REDUCE_PARTS)
    ]

    def finish_modulation():
        layer_load.wait()
        ids = lax.broadcasted_iota(jnp.int32, (8, w_layer.shape[0]), 1)
        chosen = (ids == section_layer[pipe]).astype(jnp.bfloat16)
        layer = jnp.dot(chosen, w_layer[...], preferred_element_type=jnp.float32)
        modulation[...] = mod_total[...] + layer[:clips]

    def rotary_tables():
        cells = jnp.broadcast_to(token_cell[...].astype(jnp.float32), (HEAD, tokens)).T
        columns[...] = cells
        part = 64

        def step(i, carry):
            at = pl.ds(pl.multiple_of(i * part, part), part)
            cell = columns[at].astype(jnp.int32)
            entry = lax.broadcasted_iota(jnp.int32, (part, HEAD), 1)
            pair_id = entry & (HEAD // 2 - 1)
            place = jnp.where(
                pair_id < TIME_PAIRS,
                cell // (GRID_H * GRID_W),
                jnp.where(pair_id < TIME_PAIRS + SPACE_PAIRS, lax.rem(cell // GRID_W, GRID_H), lax.rem(cell, GRID_W)),
            )
            turn = place.astype(jnp.float32) * rates[1:2, :HEAD]
            cos_ref[at] = jnp.cos(turn)
            sin_ref[at] = jnp.where(entry < HEAD // 2, -1.0, 1.0) * jnp.sin(turn)
            return carry

        lax.fori_loop(0, tokens // part, step, 0)

    def norm_block(m, owner):
        shift = modulation[pl.ds(m, 1), 0:width]
        scale = 1.0 + modulation[pl.ds(m, 1), width : 2 * width]

        def step(i, carry):
            at = pl.ds(pl.multiple_of(owner * rows + i * CHUNK, CHUNK), CHUNK)
            values = gathered[m, at].astype(jnp.float32)
            center = values - jnp.mean(values, -1, keepdims=True)
            spread = jnp.mean(center * center, -1, keepdims=True)
            normed[m, at] = (center * lax.rsqrt(spread + 1e-06) * scale + shift).astype(jnp.bfloat16)
            return carry

        lax.fori_loop(0, rows // CHUNK, step, 0, unroll=True)

    def project(m, first, last):
        raw[:, first * local_cols : last * local_cols] = jnp.dot(
            normed[m], w_all[:, first * local_cols : last * local_cols], preferred_element_type=jnp.float32
        )

    stat_sends = [
        [
            remote(stat_own.at[m], stat_got.at[m, s - 1], clips * PARTS * PER_PART + m * STATS + s - 1, ctx_peer(s))
            for s in range(1, CTX)
        ]
        for m in range(clips)
    ]

    def start_stats(m):
        q_raw = raw[:, 0:local_cols]
        k_raw = raw[:, local_cols : 2 * local_cols]
        q_sum = jnp.sum(q_raw * q_raw, -1, keepdims=True)
        k_sum = jnp.sum(k_raw * k_raw, -1, keepdims=True)
        lane = lax.broadcasted_iota(jnp.int32, (tokens, HEAD), 1)
        both = jnp.where(lane == 0, q_sum, k_sum)
        stat_own[m] = both.T[0:2]
        for copy in stat_sends[m]:
            copy.start()

    def finish_stats(m):
        total = stat_own[m]
        for s, copy in enumerate(stat_sends[m]):
            copy.wait_recv()
            total = total + stat_got[m, s]
        inverse = lax.rsqrt(total / width + 1e-06)
        columns[...] = jnp.concatenate([inverse, jnp.zeros((HEAD - 2, tokens), jnp.float32)], 0).T

    def rope(m):
        def step(h, carry):
            for kind, (gain, target) in enumerate(((q_gain, heads_q), (k_gain, heads_k))):
                here = pl.ds(pl.multiple_of(h * HEAD, HEAD), HEAD)
                there = pl.ds(pl.multiple_of(kind * local_cols + h * HEAD, HEAD), HEAD)
                value = raw[:, there] * columns[:, kind : kind + 1] * gain[:, here]
                turned = value * cos_ref[...] + pltpu.roll(value, HEAD // 2, 1) * sin_ref[...]
                target[:, here] = turned.astype(jnp.bfloat16)
            return carry

        lax.fori_loop(0, local_heads, step, 0)
        heads_v[...] = raw[:, 2 * local_cols : 3 * local_cols].astype(jnp.bfloat16)

    q_rows = 256

    def attend(m, head, heads=1):
        def step(i, carry):
            h, r = i // (tokens // q_rows), lax.rem(i, tokens // q_rows)
            here = pl.ds(pl.multiple_of(h * HEAD, HEAD), HEAD)
            at = pl.ds(pl.multiple_of(r * q_rows, q_rows), q_rows)
            scores = lax.dot_general(
                heads_q[at, here], heads_k[:, here], (((1,), (1,)), ((), ())), preferred_element_type=jnp.float32
            ) * HEAD ** (-0.5)
            scores = scores - jnp.max(scores, -1, keepdims=True)
            weights = jnp.exp(scores)
            total = jnp.sum(weights, -1, keepdims=True)
            mixed = jnp.dot(weights.astype(jnp.bfloat16), heads_v[:, here], preferred_element_type=jnp.float32)
            attended[at, here] = (mixed / total).astype(jnp.bfloat16)
            return carry

        lax.fori_loop(head * (tokens // q_rows), (head + heads) * (tokens // q_rows), step, 0)

    out_cols = 512

    def project_out(m, part, parts):
        first, last = (width // out_cols // parts * i for i in (part, part + 1))

        def step(i, carry):
            cols = pl.ds(pl.multiple_of(i * out_cols, out_cols), out_cols)
            partial[m, :, cols] = jnp.dot(
                attended[...], w_out[:, cols], preferred_element_type=jnp.float32
            ).astype(jnp.bfloat16)
            return carry

        lax.fori_loop(first, last, step, 0)

    def mod_slice(ref, index):
        return ref.at[:, pl.ds(pl.multiple_of(index * mod_cols, 128), mod_cols)]

    mod_a = [
        remote(
            mod_slice(mod_part, lax.rem(ctx + s, CTX)), mod_got_a.at[s - 1], s - 1, ctx_peer(s), mod_send, mod_recv
        )
        for s in range(1, CTX)
    ]
    number = CTX - 1
    mod_b = [
        remote(mod_sum.at[0], mod_got_b.at[s - 1], number + s - 1, depth_peer(s), mod_send, mod_recv)
        for s in range(1, depth_pipe)
    ]
    number += depth_pipe - 1
    mod_c = [
        remote(mod_sum.at[1], mod_got_c.at[s - 1], number + s - 1, quad_peer(s), mod_send, mod_recv)
        for s in range(1, lanes_pipe)
    ]
    number += lanes_pipe - 1
    mod_d = [
        remote(mod_slice(mod_total, ctx), mod_slice(mod_total, ctx), number + s - 1, ctx_peer(s), mod_send, mod_recv)
        for s in range(1, CTX)
    ]
    own_cols = pl.ds(pl.multiple_of(ctx * mod_cols, 128), mod_cols)

    def summed(value, copies, got):
        for i, copy in enumerate(copies):
            copy.wait_recv()
            value = value + got[i]
        return value

    for copy in mod_a:
        copy.start()
    g0, g1 = gathers
    r0, r1 = reduces
    for gather in g0:
        gather.start()
    for copy in weights:
        copy.start()
    rotary_tables()
    mod_sum[0] = summed(mod_part[:, own_cols], mod_a, mod_got_a)
    for copy in mod_b:
        copy.start()
    g0[0].near_up()
    g0[0].near_down()
    g0[0].near_pair()
    mod_sum[1] = summed(mod_sum[0], mod_b, mod_got_b)
    for copy in mod_c:
        copy.start()
    g0[1].near_up()
    g0[1].near_down()
    g0[1].near_pair()
    g0[0].far()
    mod_total[:, own_cols] = summed(mod_sum[1], mod_c, mod_got_c)
    for copy in mod_d:
        copy.start()
    g0[1].far()
    for copy in mod_d:
        copy.wait_recv()
    finish_modulation()
    norm_block(1, ctx)
    for gather in g1:
        gather.start()
    for owner in (ctx, c_up, c_down, c_pair, c_far):
        norm_block(0, owner)
    for copy in weights:
        copy.wait()
    for gather in g0:
        gather.finish()
    for owner in (c_pair_up, c_pair_down, c_pair_far):
        norm_block(0, owner)
    project(0, 0, 2)
    g1[0].near_up()
    g1[0].near_down()
    start_stats(0)
    g1[0].near_pair()
    project(0, 2, 3)
    g1[1].near_up()
    g1[1].near_down()
    finish_stats(0)
    g1[1].near_pair()
    rope(0)
    g1[0].far()
    attend(0, 0, 3)
    project_out(0, 0, 2)
    g1[1].far()
    r0[0].start()
    project_out(0, 1, 2)
    r0[1].start()
    for gather in g1:
        gather.finish()
    project(1, 0, 2)
    r0[0].add_pair()
    start_stats(1)
    project(1, 2, 3)
    r0[0].add_far()
    r0[1].add_pair()
    r0[0].add_cross()
    finish_stats(1)
    rope(1)
    r0[0].add_near()
    attend(1, 0)
    r0[1].add_far()
    attend(1, 1)
    r0[1].add_cross()
    attend(1, 2)
    project_out(1, 0, 3)
    r1[0].start()
    project_out(1, 1, 3)
    r1[1].start()
    r0[0].last()
    project_out(1, 2, 3)
    r1[2].start()
    r0[1].add_near()
    r1[0].add_pair()
    r1[0].add_far()
    r1[1].add_pair()
    r1[0].add_cross()
    r1[2].add_pair()
    r1[1].add_far()
    r1[1].add_cross()
    r0[1].last()
    r1[2].add_far()
    r1[2].add_cross()
    for reduce in r1:
        reduce.add_near()
    for reduce in r1:
        reduce.last()

    for gather in g0 + g1:
        gather.drain()
    every = r0 + r1
    for reduce in every:
        reduce.drain()
    for copy in mod_a + mod_b + mod_c + mod_d:
        copy.wait_send()
    for sends in stat_sends:
        for copy in sends:
            copy.wait_send()

    @pl.when(pipe < pipe_count - 1)
    def _():
        for reduce in every:
            reduce.hand.wait_send()

    @pl.when(pipe > 0)
    def _():
        for reduce in every:
            reduce.hand.wait_recv()

    @pl.when(pipe == 0)
    def _():
        out_ref[...] = jnp.zeros_like(out_ref)


def shards(
    inflow,
    patches,
    patch_weight,
    timesteps,
    time_weight,
    mod_weight,
    layer_table,
    section_layer,
    token_cell,
    q_weight,
    k_weight,
    v_weight,
    out_weight,
    q_gain,
    k_gain,
):
    clips, rows, width = inflow.shape[1:]
    local_cols = q_weight.shape[2]
    tokens = rows * CTX
    pipe_count = lax.axis_size("pipe")
    smem = pl.BlockSpec(memory_space=pltpu.SMEM)
    vmem = pl.BlockSpec(memory_space=pltpu.VMEM)
    anywhere = pl.BlockSpec(memory_space=pl.ANY)
    mod_width = mod_weight.shape[1]
    freq_count = time_weight.shape[0]
    time_cols = 32 * mod_weight.shape[0]
    mod_cols = mod_width // CTX
    lanes_pipe = min(4, pipe_count)
    depth_pipe = pipe_count // lanes_pipe
    mod_copies = 2 * (CTX - 1) + depth_pipe - 1 + lanes_pipe - 1
    bf16, f32 = jnp.bfloat16, jnp.float32
    handed = pl.pallas_call(
        functools.partial(section_kernel, pipe_count),
        out_shape=jax.ShapeDtypeStruct((clips, rows, width), bf16),
        in_specs=[smem, smem] + [anywhere] * 4 + [vmem, anywhere, vmem, vmem] + [anywhere] * 4 + [vmem, vmem],
        out_specs=vmem,
        scratch_shapes=[
            pltpu.VMEM((clips, tokens, width), bf16),
            pltpu.VMEM((clips, tokens, width), bf16),
            pltpu.VMEM((width, 3 * local_cols), bf16),
            pltpu.VMEM((local_cols, width), bf16),
            pltpu.VMEM((tokens, 3 * local_cols), f32),
            pltpu.VMEM((tokens, local_cols), bf16),
            pltpu.VMEM((tokens, local_cols), bf16),
            pltpu.VMEM((tokens, local_cols), bf16),
            pltpu.VMEM((tokens, local_cols), bf16),
            pltpu.VMEM((clips, tokens, width), bf16),
            pltpu.VMEM((clips, 6, rows, width), bf16),
            pltpu.VMEM((clips, 2, rows // 2, width), bf16),
            pltpu.VMEM((clips, 2, rows, width), bf16),
            pltpu.VMEM((clips, 2, tokens), f32),
            pltpu.VMEM((clips, CTX - 1, 2, tokens), f32),
            pltpu.VMEM((tokens, HEAD), f32),
            pltpu.VMEM((2, clips, mod_cols), f32),
            pltpu.VMEM((CTX - 1, clips, mod_cols), f32),
            pltpu.VMEM((max(depth_pipe - 1, 1), clips, mod_cols), f32),
            pltpu.VMEM((max(lanes_pipe - 1, 1), clips, mod_cols), f32),
            pltpu.VMEM((clips, mod_width), f32),
            pltpu.VMEM((clips, mod_width), f32),
            pltpu.VMEM((clips, mod_width), f32),
            pltpu.VMEM((tokens, HEAD), f32),
            pltpu.VMEM((tokens, HEAD), f32),
            pltpu.VMEM((freq_count, time_cols), bf16),
            pltpu.VMEM(patch_weight.shape, bf16),
            pltpu.VMEM(layer_table.shape, bf16),
            pltpu.VMEM(patches.shape, bf16),
            pltpu.SemaphoreType.DMA((clips * (PARTS * PER_PART + STATS),)),
            pltpu.SemaphoreType.DMA((clips * (PARTS * PER_PART + STATS),)),
            pltpu.SemaphoreType.DMA((mod_copies,)),
            pltpu.SemaphoreType.DMA((mod_copies,)),
            pltpu.SemaphoreType.DMA((clips + 8,)),
        ],
        compiler_params=pltpu.CompilerParams(
            collective_id=0, has_side_effects=True, vmem_limit_bytes=56 * 2**20
        ),
        cost_estimate=pl.CostEstimate(
            flops=2 * clips * tokens * width * local_cols * 4, bytes_accessed=4 * width * local_cols * 2, transcendentals=0
        ),
    )(
        timesteps,
        section_layer,
        inflow,
        patches,
        patch_weight,
        time_weight,
        mod_weight,
        layer_table,
        token_cell[None],
        rate_rows(freq_count),
        q_weight,
        k_weight,
        v_weight,
        out_weight,
        q_gain,
        k_gain,
    )
    return handed[None]


def solution(mesh):
    placed = (
        P("pipe", None, "ctx", None),
        P(None, "ctx", None),
        P(),
        P(),
        P(),
        P(("pipe", "ctx"), None),
        P(),
        P(),
        P(),
        P("pipe", None, "ctx"),
        P("pipe", None, "ctx"),
        P("pipe", None, "ctx"),
        P("pipe", "ctx", None),
        P("pipe", "ctx"),
        P("pipe", "ctx"),
    )
    return jax.shard_map(
        shards, mesh=mesh, in_specs=placed, out_specs=P("pipe", None, "ctx", None), check_vma=False
    )
```

```python
import functools

import jax
import jax.numpy as jnp
import numpy as np
from jax import lax
from jax.experimental import pallas as pl
from jax.experimental.pallas import tpu as pltpu
from jax.sharding import PartitionSpec as P

HEAD = 128
GRID_H = 8
GRID_W = 16
MESH = pl.DeviceIdType.MESH
CTX = 8
CHUNK = 16
SPACE_PAIRS = HEAD // 6
TIME_PAIRS = HEAD // 2 - 2 * SPACE_PAIRS

GATHER_PARTS = (2, 2)
REDUCE_PARTS = (2, 2)
PARTS = 2
GATHER = 0
REDUCE = 10
PER_PART = 21
STATS = CTX - 1


def column_parts(width, parts):
    span = width // parts
    cross = span // 6 // 128 * 128
    return [
        (slice(p * span, (p + 1) * span), slice(p * span, (p + 1) * span - cross), slice((p + 1) * span - cross, (p + 1) * span))
        for p in range(parts)
    ]


def rate_rows(freq_count):
    half_freq = freq_count // 2
    time_rates = 10000.0 ** (-np.arange(half_freq) / half_freq)
    half_size = HEAD // 2
    pair_ids = np.arange(half_size)
    exponent = np.where(
        pair_ids < TIME_PAIRS,
        pair_ids / TIME_PAIRS,
        np.where(
            pair_ids < TIME_PAIRS + SPACE_PAIRS,
            (pair_ids - TIME_PAIRS) / SPACE_PAIRS,
            (pair_ids - TIME_PAIRS - SPACE_PAIRS) / SPACE_PAIRS,
        ),
    )
    table = np.zeros((8, max(freq_count, HEAD)), np.float32)
    table[0, :freq_count] = np.concatenate([time_rates, time_rates])
    table[1, :HEAD] = np.concatenate([10000.0 ** (-exponent)] * 2)
    return table


def section_kernel(
    pipe_count,
    timesteps,
    section_layer,
    inflow,
    patches,
    patch_weight,
    time_weight,
    mod_weight,
    layer_table,
    token_cell,
    rates,
    q_weight,
    k_weight,
    v_weight,
    out_weight,
    q_gain,
    k_gain,
    out_ref,
    gathered,
    normed,
    w_all,
    w_out,
    raw,
    heads_q,
    heads_k,
    heads_v,
    attended,
    partial,
    got_full,
    got_half,
    got_cross,
    stat_own,
    stat_got,
    columns,
    mod_sum,
    mod_got_a,
    mod_got_b,
    mod_got_c,
    mod_total,
    mod_part,
    modulation,
    cos_ref,
    sin_ref,
    w_time,
    w_patch,
    w_layer,
    patch_rows,
    send_sems,
    recv_sems,
    mod_send,
    mod_recv,
    load_sems,
):
    clips, rows, width = inflow.shape[1:]
    local_cols = q_weight.shape[2]
    local_heads = local_cols // HEAD
    tokens = rows * CTX
    mod_cols = mod_part.shape[1] // CTX
    lanes_pipe = min(4, pipe_count)
    depth_pipe = pipe_count // lanes_pipe

    pipe = lax.axis_index("pipe")
    ctx = lax.axis_index("ctx")
    y, side = ctx // 2, ctx % 2

    def at_ctx(row, col):
        return lax.rem(row + 4, 4) * 2 + col

    c_up, c_down, c_far = at_ctx(y + 1, side), at_ctx(y - 1, side), at_ctx(y + 2, side)
    c_pair = at_ctx(y, 1 - side)
    c_pair_up, c_pair_down, c_pair_far = (
        at_ctx(y + 1, 1 - side),
        at_ctx(y - 1, 1 - side),
        at_ctx(y + 2, 1 - side),
    )
    up, down, pair = (pipe, c_up), (pipe, c_down), (pipe, c_pair)

    core = lax.rem(pipe, 2)
    if pipe_count >= 4:
        z = lax.rem(pipe // 2, depth_pipe)
        x_lo = pipe // (2 * depth_pipe)

        def depth_peer(step):
            return ((x_lo * depth_pipe + lax.rem(z + step, depth_pipe)) * 2 + core, ctx)

        def quad_peer(step):
            there = lax.rem(x_lo * 2 + core + step, 4)
            return (((there // 2) * depth_pipe + z) * 2 + lax.rem(there, 2), ctx)

    else:

        def depth_peer(step):
            return (pipe, ctx)

        def quad_peer(step):
            return (lax.rem(pipe + step, lanes_pipe), ctx)

    def ctx_peer(step):
        return (pipe, lax.rem(ctx + step, CTX))

    after = (lax.rem(pipe + 1, pipe_count), ctx)
    before = (lax.rem(pipe + pipe_count - 1, pipe_count), ctx)

    def own_rows(m):
        return gathered.at[m, pl.ds(pl.multiple_of(ctx * rows, rows), rows)]

    loads = [pltpu.make_async_copy(inflow.at[0, m], own_rows(m), load_sems.at[m]) for m in range(clips)]
    share = mod_weight.shape[0]
    time_cols = w_time.shape[1]
    shares = time_cols // share
    rank = pipe * CTX + ctx
    time_load = pltpu.make_async_copy(
        time_weight.at[:, pl.ds(pl.multiple_of((rank // shares) * time_cols, 128), time_cols)],
        w_time,
        load_sems.at[clips],
    )
    layer_load = pltpu.make_async_copy(layer_table, w_layer, load_sems.at[clips + 1])
    patch_loads = [
        pltpu.make_async_copy(patch_weight, w_patch, load_sems.at[clips + 2]),
        pltpu.make_async_copy(patches, patch_rows, load_sems.at[clips + 3]),
    ]
    weights = [
        pltpu.make_async_copy(w.at[0], w_all.at[:, pl.ds(i * local_cols, local_cols)], load_sems.at[clips + 4 + i])
        for i, w in enumerate((q_weight, k_weight, v_weight))
    ] + [pltpu.make_async_copy(out_weight.at[0], w_out, load_sems.at[clips + 7])]

    @pl.when(pipe > 0)
    def _():
        for copy in loads:
            copy.start()

    @pl.when(pipe == 0)
    def _():
        for copy in patch_loads:
            copy.start()

    time_load.start()
    layer_load.start()

    greeted = (
        [ctx_peer(s) for s in range(1, CTX)]
        + [depth_peer(s) for s in range(1, depth_pipe)]
        + [quad_peer(s) for s in range(1, lanes_pipe)]
        + [after, before]
    )
    barrier = pltpu.get_barrier_semaphore()
    for peer in greeted:
        pl.semaphore_signal(barrier, inc=1, device_id=peer, device_id_type=MESH)

    lane = lax.broadcasted_iota(jnp.int32, (8, rates.shape[1]), 1)
    line = lax.broadcasted_iota(jnp.int32, (8, rates.shape[1]), 0)
    steps = jnp.where(line == 0, timesteps[0], timesteps[1]).astype(jnp.float32)
    angles = steps * rates[0:1, :]
    features = jnp.where(lane < rates.shape[1] // 2, jnp.cos(angles), jnp.sin(angles)).astype(jnp.bfloat16)
    time_load.wait()
    time_hidden = jax.nn.silu(
        jnp.dot(features, w_time[...], preferred_element_type=jnp.float32)
    ).astype(jnp.bfloat16)
    first = lax.rem(rank, shares) * share
    picked = lax.broadcasted_iota(jnp.int32, (time_cols, 128), 0) - first
    picks = (picked == lax.broadcasted_iota(jnp.int32, (time_cols, 128), 1)).astype(jnp.bfloat16)
    time_piece = jnp.dot(time_hidden, picks, preferred_element_type=jnp.float32).astype(jnp.bfloat16)
    mod_part[...] = jnp.dot(
        time_piece[:, :share], mod_weight[...], preferred_element_type=jnp.float32
    )[:clips]

    @pl.when(pipe == 0)
    def _():
        for copy in patch_loads:
            copy.wait()
        for m in range(clips):
            embedded = jnp.dot(patch_rows[m], w_patch[...], preferred_element_type=jnp.float32)
            gathered[m, pl.ds(pl.multiple_of(ctx * rows, rows), rows)] = embedded.astype(jnp.bfloat16)

    @pl.when(pipe > 0)
    def _():
        for copy in loads:
            copy.wait()

    pl.semaphore_wait(barrier, len(greeted))

    def remote(src, dst, number, peer, sends=send_sems, recvs=recv_sems):
        return pltpu.make_async_remote_copy(
            src_ref=src,
            dst_ref=dst,
            send_sem=sends.at[number],
            recv_sem=recvs.at[number],
            device_id=peer,
            device_id_type=MESH,
        )

    def block(ref, m, owner, first=0, count=rows, cols=slice(None)):
        return ref.at[m, pl.ds(pl.multiple_of(owner * rows + first, 16), count), cols]

    half = rows // 2
    seen = set()

    def arrived(*copies):
        for copy in copies:
            if id(copy) not in seen:
                seen.add(id(copy))
                copy.wait_recv()

    class Gather:
        def __init__(self, m, part, columns_of):
            base = (m * PARTS + part) * PER_PART + GATHER
            whole, straight, crossing = columns_of

            def send(owner, number, peer, first=0, count=rows, cols=whole):
                piece = block(gathered if m == 0 else normed, m, owner, first, count, cols)
                return remote(piece, piece, base + number, peer)

            self.own = [send(ctx, 0, up), send(ctx, 1, down), send(ctx, 2, pair)]
            self.far_up = send(c_down, 3, up, 0, half)
            self.far_down = send(c_up, 4, down, half, half)
            self.other_up = send(c_pair, 5, up, cols=straight)
            self.other_down = send(c_pair, 6, down, cols=straight)
            self.far_pair = send(c_far, 7, pair)
            self.cross_up = send(c_down, 8, pair, cols=crossing)
            self.cross_down = send(c_up, 9, pair, cols=crossing)
            self.rest = [self.other_up, self.other_down, self.cross_up, self.cross_down, self.far_pair]
            self.all = self.own + [self.far_up, self.far_down] + self.rest

        def start(self):
            self.own[0].start()
            self.own[1].start()

        def start_pair(self):
            self.own[2].start()

        def near_up(self):
            arrived(self.own[0])
            self.far_up.start()
            self.cross_up.start()

        def near_down(self):
            arrived(self.own[1])
            self.far_down.start()
            self.cross_down.start()

        def near_pair(self):
            arrived(self.own[2])
            self.other_up.start()
            self.other_down.start()

        def far(self):
            arrived(self.far_up)
            arrived(self.far_down)
            self.far_pair.start()

        def finish(self):
            arrived(*self.own, self.far_up, self.far_down, *self.rest)

        def drain(self):
            for copy in self.all:
                copy.wait_send()

    gathers = [
        [Gather(m, i, columns_of) for i, columns_of in enumerate(column_parts(width, parts))]
        for m, parts in enumerate(GATHER_PARTS)
    ]

    def add_into(m, owner, first, count, sources, cols):
        def step(i, carry):
            at = pl.ds(pl.multiple_of(owner * rows + first + i * CHUNK, CHUNK), CHUNK)
            total = partial[m, at, cols].astype(jnp.float32)
            for source in sources:
                total = total + source[pl.ds(i * CHUNK, CHUNK), cols].astype(jnp.float32)
            partial[m, at, cols] = total.astype(jnp.bfloat16)
            return carry

        lax.fori_loop(0, count // CHUNK, step, 0)

    class Reduce:
        def __init__(self, m, part, columns_of):
            self.m = m
            base = (m * PARTS + part) * PER_PART + REDUCE
            self.whole, self.straight, self.crossing = whole, straight, crossing = columns_of

            def send(owner, number, peer, into, first=0, count=rows, cols=whole):
                return remote(
                    block(partial, m, owner, first, count, cols), into.at[:, cols], base + number, peer
                )

            self.full = full = [got_full.at[m, i] for i in range(6)]
            self.halves = halves = [got_half.at[m, i] for i in range(2)]
            self.crossed = crossed = [got_cross.at[m, i] for i in range(2)]
            self.far_pair = send(c_pair_far, 0, pair, full[0])
            self.other_up = send(c_pair_up, 1, up, full[1], cols=straight)
            self.other_down = send(c_pair_down, 2, down, full[2], cols=straight)
            self.cross_up = send(c_pair_up, 8, pair, crossed[0], cols=crossing)
            self.cross_down = send(c_pair_down, 9, pair, crossed[1], cols=crossing)
            self.hand = remote(block(partial, m, ctx, cols=whole), out_ref.at[m, :, whole], base + 10, after)
            self.far_down = send(c_far, 3, down, halves[0], 0, half)
            self.far_up = send(c_far, 4, up, halves[1], half, half)
            self.near_down = send(c_down, 5, down, full[3])
            self.near_up = send(c_up, 6, up, full[4])
            self.pair = send(c_pair, 7, pair, full[5])
            self.all = [
                self.far_pair,
                self.other_up,
                self.other_down,
                self.far_down,
                self.far_up,
                self.near_down,
                self.near_up,
                self.pair,
                self.cross_up,
                self.cross_down,
            ]

        def start(self):
            self.other_up.start()
            self.other_down.start()

        def start_far(self):
            self.far_pair.start()

        def start_cross(self):
            self.cross_up.start()
            self.cross_down.start()

        def add_far(self):
            arrived(self.far_pair)
            add_into(self.m, c_far, 0, rows, [self.full[0]], self.whole)
            self.far_down.start()
            self.far_up.start()

        def add_pair(self):
            arrived(self.other_up)
            arrived(self.other_down)
            add_into(self.m, c_pair, 0, rows, self.full[1:3], self.straight)
            self.pair.start()

        def add_cross(self):
            arrived(self.cross_up)
            arrived(self.cross_down)
            add_into(self.m, c_up, 0, rows, [self.crossed[0]], self.crossing)
            add_into(self.m, c_down, 0, rows, [self.crossed[1]], self.crossing)

        def add_near(self):
            arrived(self.far_down)
            add_into(self.m, c_down, 0, half, [self.halves[0]], self.whole)
            self.near_down.start()
            arrived(self.far_up)
            add_into(self.m, c_up, half, half, [self.halves[1]], self.whole)
            self.near_up.start()

        def last(self):
            arrived(self.near_down)
            arrived(self.near_up)
            arrived(self.pair)
            m = self.m
            cols = self.whole
            gate = modulation[pl.ds(m, 1), 2 * width + cols.start : 2 * width + cols.stop]

            def step(i, carry):
                at = pl.ds(pl.multiple_of(ctx * rows + i * CHUNK, CHUNK), CHUNK)
                here = pl.ds(i * CHUNK, CHUNK)
                branch = partial[m, at, cols].astype(jnp.float32)
                for source in self.full[3:]:
                    branch = branch + source[here, cols].astype(jnp.float32)
                result = gathered[m, at, cols].astype(jnp.float32) + gate * branch
                partial[m, at, cols] = result.astype(jnp.bfloat16)
                return carry

            lax.fori_loop(0, rows // CHUNK, step, 0)

            @pl.when(pipe < pipe_count - 1)
            def _():
                self.hand.start()

        def drain(self):
            for copy in self.all:
                copy.wait_send()

    reduces = [
        [Reduce(m, i, columns_of) for i, columns_of in enumerate(column_parts(width, parts))]
        for m, parts in enumerate(REDUCE_PARTS)
    ]

    def finish_modulation():
        layer_load.wait()
        ids = lax.broadcasted_iota(jnp.int32, (8, w_layer.shape[0]), 1)
        chosen = (ids == section_layer[pipe]).astype(jnp.bfloat16)
        layer = jnp.dot(chosen, w_layer[...], preferred_element_type=jnp.float32)
        modulation[...] = mod_total[...] + layer[:clips]

    def rotary_tables():
        cells = jnp.broadcast_to(token_cell[...].astype(jnp.float32), (HEAD, tokens)).T
        columns[...] = cells
        part = 64

        def step(i, carry):
            at = pl.ds(pl.multiple_of(i * part, part), part)
            cell = columns[at].astype(jnp.int32)
            entry = lax.broadcasted_iota(jnp.int32, (part, HEAD), 1)
            pair_id = entry & (HEAD // 2 - 1)
            place = jnp.where(
                pair_id < TIME_PAIRS,
                cell // (GRID_H * GRID_W),
                jnp.where(pair_id < TIME_PAIRS + SPACE_PAIRS, lax.rem(cell // GRID_W, GRID_H), lax.rem(cell, GRID_W)),
            )
            turn = place.astype(jnp.float32) * rates[1:2, :HEAD]
            cos_ref[at] = jnp.cos(turn)
            sin_ref[at] = jnp.where(entry < HEAD // 2, -1.0, 1.0) * jnp.sin(turn)
            return carry

        lax.fori_loop(0, tokens // part, step, 0)

    def norm_block(m, owner):
        shift = modulation[pl.ds(m, 1), 0:width]
        scale = 1.0 + modulation[pl.ds(m, 1), width : 2 * width]

        def step(i, carry):
            at = pl.ds(pl.multiple_of(owner * rows + i * CHUNK, CHUNK), CHUNK)
            values = gathered[m, at].astype(jnp.float32)
            center = values - jnp.mean(values, -1, keepdims=True)
            spread = jnp.mean(center * center, -1, keepdims=True)
            normed[m, at] = (center * lax.rsqrt(spread + 1e-06) * scale + shift).astype(jnp.bfloat16)
            return carry

        lax.fori_loop(0, rows // CHUNK, step, 0, unroll=True)

    def project(m):
        raw[...] = jnp.dot(normed[m], w_all[:, : 2 * local_cols], preferred_element_type=jnp.float32)

    def project_values(m):
        heads_v[...] = jnp.dot(
            normed[m], w_all[:, 2 * local_cols :], preferred_element_type=jnp.float32
        ).astype(jnp.bfloat16)

    stat_sends = [
        [
            remote(stat_own.at[m], stat_got.at[m, s - 1], clips * PARTS * PER_PART + m * STATS + s - 1, ctx_peer(s))
            for s in range(1, CTX)
        ]
        for m in range(clips)
    ]

    def start_stats(m):
        q_raw = raw[:, 0:local_cols]
        k_raw = raw[:, local_cols : 2 * local_cols]
        q_sum = jnp.sum(q_raw * q_raw, -1, keepdims=True)
        k_sum = jnp.sum(k_raw * k_raw, -1, keepdims=True)
        lane = lax.broadcasted_iota(jnp.int32, (tokens, HEAD), 1)
        both = jnp.where(lane == 0, q_sum, k_sum)
        stat_own[m] = both.T[0:2]
        for copy in stat_sends[m]:
            copy.start()

    def finish_stats(m):
        total = stat_own[m]
        for s, copy in enumerate(stat_sends[m]):
            copy.wait_recv()
            total = total + stat_got[m, s]
        inverse = lax.rsqrt(total / width + 1e-06)
        columns[...] = jnp.concatenate([inverse, jnp.zeros((HEAD - 2, tokens), jnp.float32)], 0).T

    def rope(m):
        def step(h, carry):
            for kind, (gain, target) in enumerate(((q_gain, heads_q), (k_gain, heads_k))):
                here = pl.ds(pl.multiple_of(h * HEAD, HEAD), HEAD)
                there = pl.ds(pl.multiple_of(kind * local_cols + h * HEAD, HEAD), HEAD)
                value = raw[:, there] * columns[:, kind : kind + 1] * gain[:, here]
                turned = value * cos_ref[...] + pltpu.roll(value, HEAD // 2, 1) * sin_ref[...]
                target[:, here] = turned.astype(jnp.bfloat16)
            return carry

        lax.fori_loop(0, local_heads, step, 0)

    q_rows = 256

    def attend(m, head, heads=1):
        def step(i, carry):
            h, r = i // (tokens // q_rows), lax.rem(i, tokens // q_rows)
            here = pl.ds(pl.multiple_of(h * HEAD, HEAD), HEAD)
            at = pl.ds(pl.multiple_of(r * q_rows, q_rows), q_rows)
            scores = lax.dot_general(
                heads_q[at, here], heads_k[:, here], (((1,), (1,)), ((), ())), preferred_element_type=jnp.float32
            ) * HEAD ** (-0.5)
            scores = scores - jnp.max(scores, -1, keepdims=True)
            weights = jnp.exp(scores)
            total = jnp.sum(weights, -1, keepdims=True)
            mixed = jnp.dot(weights.astype(jnp.bfloat16), heads_v[:, here], preferred_element_type=jnp.float32)
            attended[at, here] = (mixed / total).astype(jnp.bfloat16)
            return carry

        lax.fori_loop(head * (tokens // q_rows), (head + heads) * (tokens // q_rows), step, 0)

    out_cols = 512

    def project_out(m, part, parts):
        first, last = (width // out_cols // parts * i for i in (part, part + 1))

        def step(i, carry):
            cols = pl.ds(pl.multiple_of(i * out_cols, out_cols), out_cols)
            partial[m, :, cols] = jnp.dot(
                attended[...], w_out[:, cols], preferred_element_type=jnp.float32
            ).astype(jnp.bfloat16)
            return carry

        lax.fori_loop(first, last, step, 0)

    def mod_slice(ref, index):
        return ref.at[:, pl.ds(pl.multiple_of(index * mod_cols, 128), mod_cols)]

    mod_a = [
        remote(
            mod_slice(mod_part, lax.rem(ctx + s, CTX)), mod_got_a.at[s - 1], s - 1, ctx_peer(s), mod_send, mod_recv
        )
        for s in range(1, CTX)
    ]
    number = CTX - 1
    mod_b = [
        remote(mod_sum.at[1], mod_got_b.at[s - 1], number + s - 1, depth_peer(s), mod_send, mod_recv)
        for s in range(1, depth_pipe)
    ]
    number += depth_pipe - 1
    mod_c = [
        remote(mod_sum.at[0], mod_got_c.at[s - 1], number + s - 1, quad_peer(s), mod_send, mod_recv)
        for s in range(1, lanes_pipe)
    ]
    number += lanes_pipe - 1
    mod_d = [
        remote(mod_slice(mod_total, ctx), mod_slice(mod_total, ctx), number + s - 1, ctx_peer(s), mod_send, mod_recv)
        for s in range(1, CTX)
    ]
    own_cols = pl.ds(pl.multiple_of(ctx * mod_cols, 128), mod_cols)

    def summed(value, copies, got):
        for i, copy in enumerate(copies):
            copy.wait_recv()
            value = value + got[i]
        return value

    g0, g1 = gathers
    r0, r1 = reduces
    for copy in mod_a:
        copy.start()
    g0[1].start()
    g0[1].start_pair()
    g0[0].start()
    mod_sum[0] = summed(mod_part[:, own_cols], mod_a, mod_got_a)
    for copy in mod_c:
        copy.start()
    g0[0].start_pair()
    g0[1].near_down()
    mod_sum[1] = summed(mod_sum[0], mod_c, mod_got_c)
    for copy in mod_b:
        copy.start()
    g0[1].near_up()
    g0[0].near_down()
    g0[0].near_up()
    mod_total[:, own_cols] = summed(mod_sum[1], mod_b, mod_got_b)
    for copy in mod_d:
        copy.start()
    g0[1].far()
    g0[1].near_pair()
    g0[0].near_pair()
    g0[0].far()
    for copy in weights:
        copy.start()
    rotary_tables()
    for copy in mod_d:
        copy.wait_recv()
    finish_modulation()
    arrived(g0[0].own[1], g0[1].own[1])
    norm_block(0, c_up)
    norm_block(1, ctx)
    g1[1].start()
    g1[1].start_pair()
    arrived(g0[0].own[0], g0[1].own[0])
    norm_block(0, c_down)
    arrived(g0[0].own[2], g0[1].own[2])
    norm_block(0, c_pair)
    arrived(g0[0].far_up, g0[0].far_down, g0[1].far_up, g0[1].far_down)
    norm_block(0, c_far)
    g1[0].start()
    arrived(g0[0].other_up, g0[0].cross_up, g0[1].other_up, g0[1].cross_up)
    norm_block(0, c_pair_down)
    norm_block(0, ctx)
    arrived(g0[0].other_down, g0[0].cross_down, g0[1].other_down, g0[1].cross_down)
    norm_block(0, c_pair_up)
    g1[0].start_pair()
    arrived(g0[0].far_pair, g0[1].far_pair)
    norm_block(0, c_pair_far)
    for copy in weights:
        copy.wait()
    project(0)
    start_stats(0)
    g1[1].near_up()
    g1[1].near_down()
    g1[0].near_down()
    g1[0].near_up()
    g1[1].near_pair()
    project_values(0)
    g1[1].far()
    g1[0].near_pair()
    g1[0].far()
    finish_stats(0)
    rope(0)
    attend(0, 0)
    attend(0, 1)
    attend(0, 2)
    project_out(0, 0, 2)
    r0[0].start_far()
    r0[0].start()
    project_out(0, 1, 2)
    r0[1].start()
    r0[1].start_far()
    for gather in g1:
        gather.finish()
    project(1)
    start_stats(1)
    r0[0].start_cross()
    r0[1].start_cross()
    r0[0].add_far()
    r0[0].add_pair()
    project_values(1)
    r0[1].add_pair()
    r0[1].add_far()
    r0[0].add_cross()
    r0[0].add_near()
    r0[1].add_cross()
    finish_stats(1)
    rope(1)
    r0[1].add_near()
    attend(1, 0)
    attend(1, 1)
    attend(1, 2)
    project_out(1, 0, 2)
    r1[0].start_far()
    r1[0].start()
    project_out(1, 1, 2)
    r0[0].last()
    r1[1].start_far()
    r1[1].start()
    r0[1].last()
    r1[0].add_far()
    r1[0].start_cross()
    r1[1].start_cross()
    r1[1].add_far()
    r1[0].add_cross()
    r1[0].add_pair()
    r1[0].add_near()
    r1[1].add_pair()
    r1[1].add_cross()
    r1[1].add_near()
    r1[0].last()
    r1[1].last()

    for gather in g0 + g1:
        gather.drain()
    every = r0 + r1
    for reduce in every:
        reduce.drain()
    for copy in mod_a + mod_b + mod_c + mod_d:
        copy.wait_send()
    for sends in stat_sends:
        for copy in sends:
            copy.wait_send()

    @pl.when(pipe < pipe_count - 1)
    def _():
        for reduce in every:
            reduce.hand.wait_send()

    @pl.when(pipe > 0)
    def _():
        for reduce in every:
            reduce.hand.wait_recv()

    @pl.when(pipe == 0)
    def _():
        out_ref[...] = jnp.zeros_like(out_ref)


def shards(
    inflow,
    patches,
    patch_weight,
    timesteps,
    time_weight,
    mod_weight,
    layer_table,
    section_layer,
    token_cell,
    q_weight,
    k_weight,
    v_weight,
    out_weight,
    q_gain,
    k_gain,
):
    clips, rows, width = inflow.shape[1:]
    local_cols = q_weight.shape[2]
    tokens = rows * CTX
    pipe_count = lax.axis_size("pipe")
    smem = pl.BlockSpec(memory_space=pltpu.SMEM)
    vmem = pl.BlockSpec(memory_space=pltpu.VMEM)
    anywhere = pl.BlockSpec(memory_space=pl.ANY)
    mod_width = mod_weight.shape[1]
    freq_count = time_weight.shape[0]
    time_cols = 32 * mod_weight.shape[0]
    mod_cols = mod_width // CTX
    lanes_pipe = min(4, pipe_count)
    depth_pipe = pipe_count // lanes_pipe
    mod_copies = 2 * (CTX - 1) + depth_pipe - 1 + lanes_pipe - 1
    bf16, f32 = jnp.bfloat16, jnp.float32
    handed = pl.pallas_call(
        functools.partial(section_kernel, pipe_count),
        out_shape=jax.ShapeDtypeStruct((clips, rows, width), bf16),
        in_specs=[smem, smem] + [anywhere] * 4 + [vmem, anywhere, vmem, vmem] + [anywhere] * 4 + [vmem, vmem],
        out_specs=vmem,
        scratch_shapes=[
            pltpu.VMEM((clips, tokens, width), bf16),
            pltpu.VMEM((clips, tokens, width), bf16),
            pltpu.VMEM((width, 3 * local_cols), bf16),
            pltpu.VMEM((local_cols, width), bf16),
            pltpu.VMEM((tokens, 2 * local_cols), f32),
            pltpu.VMEM((tokens, local_cols), bf16),
            pltpu.VMEM((tokens, local_cols), bf16),
            pltpu.VMEM((tokens, local_cols), bf16),
            pltpu.VMEM((tokens, local_cols), bf16),
            pltpu.VMEM((clips, tokens, width), bf16),
            pltpu.VMEM((clips, 6, rows, width), bf16),
            pltpu.VMEM((clips, 2, rows // 2, width), bf16),
            pltpu.VMEM((clips, 2, rows, width), bf16),
            pltpu.VMEM((clips, 2, tokens), f32),
            pltpu.VMEM((clips, CTX - 1, 2, tokens), f32),
            pltpu.VMEM((tokens, HEAD), f32),
            pltpu.VMEM((2, clips, mod_cols), f32),
            pltpu.VMEM((CTX - 1, clips, mod_cols), f32),
            pltpu.VMEM((max(depth_pipe - 1, 1), clips, mod_cols), f32),
            pltpu.VMEM((max(lanes_pipe - 1, 1), clips, mod_cols), f32),
            pltpu.VMEM((clips, mod_width), f32),
            pltpu.VMEM((clips, mod_width), f32),
            pltpu.VMEM((clips, mod_width), f32),
            pltpu.VMEM((tokens, HEAD), f32),
            pltpu.VMEM((tokens, HEAD), f32),
            pltpu.VMEM((freq_count, time_cols), bf16),
            pltpu.VMEM(patch_weight.shape, bf16),
            pltpu.VMEM(layer_table.shape, bf16),
            pltpu.VMEM(patches.shape, bf16),
            pltpu.SemaphoreType.DMA((clips * (PARTS * PER_PART + STATS),)),
            pltpu.SemaphoreType.DMA((clips * (PARTS * PER_PART + STATS),)),
            pltpu.SemaphoreType.DMA((mod_copies,)),
            pltpu.SemaphoreType.DMA((mod_copies,)),
            pltpu.SemaphoreType.DMA((clips + 8,)),
        ],
        compiler_params=pltpu.CompilerParams(
            collective_id=0, has_side_effects=True, vmem_limit_bytes=56 * 2**20
        ),
        cost_estimate=pl.CostEstimate(
            flops=2 * clips * tokens * width * local_cols * 4, bytes_accessed=4 * width * local_cols * 2, transcendentals=0
        ),
    )(
        timesteps,
        section_layer,
        inflow,
        patches,
        patch_weight,
        time_weight,
        mod_weight,
        layer_table,
        token_cell[None],
        rate_rows(freq_count),
        q_weight,
        k_weight,
        v_weight,
        out_weight,
        q_gain,
        k_gain,
    )
    return handed[None]


def solution(mesh):
    placed = (
        P("pipe", None, "ctx", None),
        P(None, "ctx", None),
        P(),
        P(),
        P(),
        P(("pipe", "ctx"), None),
        P(),
        P(),
        P(),
        P("pipe", None, "ctx"),
        P("pipe", None, "ctx"),
        P("pipe", None, "ctx"),
        P("pipe", "ctx", None),
        P("pipe", "ctx"),
        P("pipe", "ctx"),
    )
    return jax.shard_map(
        shards, mesh=mesh, in_specs=placed, out_specs=P("pipe", None, "ctx", None), check_vma=False
    )
```

```python
import functools

import jax
import jax.numpy as jnp
import numpy as np
from jax import lax
from jax.experimental import pallas as pl
from jax.experimental.pallas import tpu as pltpu
from jax.sharding import PartitionSpec as P

HEAD = 128
GRID_H = 8
GRID_W = 16
MESH = pl.DeviceIdType.MESH
CTX = 8
CHUNK = 16
SPACE_PAIRS = HEAD // 6
TIME_PAIRS = HEAD // 2 - 2 * SPACE_PAIRS

GATHER_PARTS = (2, 2)
REDUCE_PARTS = (2, 2)
PARTS = 2
GATHER = 0
REDUCE = 10
PER_PART = 22
CROSSED_REDUCE = False
STATS = CTX - 1


def column_parts(width, parts, cross_share):
    span = width // parts
    cross = span // cross_share // 128 * 128
    return [
        (slice(p * span, (p + 1) * span), slice(p * span, (p + 1) * span - cross), slice((p + 1) * span - cross, (p + 1) * span))
        for p in range(parts)
    ]


def rate_rows(freq_count):
    half_freq = freq_count // 2
    time_rates = 10000.0 ** (-np.arange(half_freq) / half_freq)
    half_size = HEAD // 2
    pair_ids = np.arange(half_size)
    exponent = np.where(
        pair_ids < TIME_PAIRS,
        pair_ids / TIME_PAIRS,
        np.where(
            pair_ids < TIME_PAIRS + SPACE_PAIRS,
            (pair_ids - TIME_PAIRS) / SPACE_PAIRS,
            (pair_ids - TIME_PAIRS - SPACE_PAIRS) / SPACE_PAIRS,
        ),
    )
    table = np.zeros((8, max(freq_count, HEAD)), np.float32)
    table[0, :freq_count] = np.concatenate([time_rates, time_rates])
    table[1, :HEAD] = np.concatenate([10000.0 ** (-exponent)] * 2)
    return table


def section_kernel(
    pipe_count,
    timesteps,
    section_layer,
    inflow,
    patches,
    patch_weight,
    time_weight,
    mod_weight,
    layer_table,
    token_cell,
    rates,
    q_weight,
    k_weight,
    v_weight,
    out_weight,
    q_gain,
    k_gain,
    out_ref,
    gathered,
    normed,
    w_all,
    w_out,
    raw,
    heads_q,
    heads_k,
    heads_v,
    attended,
    partial,
    got_full,
    got_half,
    got_cross,
    stat_own,
    stat_got,
    columns,
    mod_sum,
    mod_got_a,
    mod_got_b,
    mod_got_c,
    mod_total,
    mod_part,
    modulation,
    cos_ref,
    sin_ref,
    w_time,
    w_patch,
    w_layer,
    patch_rows,
    relay,
    send_sems,
    recv_sems,
    mod_send,
    mod_recv,
    load_sems,
):
    clips, rows, width = inflow.shape[1:]
    local_cols = q_weight.shape[2]
    local_heads = local_cols // HEAD
    tokens = rows * CTX
    mod_cols = mod_part.shape[1] // CTX
    lanes_pipe = min(4, pipe_count)
    depth_pipe = pipe_count // lanes_pipe

    pipe = lax.axis_index("pipe")
    ctx = lax.axis_index("ctx")
    y, side = ctx // 2, ctx % 2

    def at_ctx(row, col):
        return lax.rem(row + 4, 4) * 2 + col

    c_up, c_down, c_far = at_ctx(y + 1, side), at_ctx(y - 1, side), at_ctx(y + 2, side)
    c_pair = at_ctx(y, 1 - side)
    c_pair_up, c_pair_down, c_pair_far = (
        at_ctx(y + 1, 1 - side),
        at_ctx(y - 1, 1 - side),
        at_ctx(y + 2, 1 - side),
    )
    up, down, pair = (pipe, c_up), (pipe, c_down), (pipe, c_pair)

    core = lax.rem(pipe, 2)
    if pipe_count >= 4:
        z = lax.rem(pipe // 2, depth_pipe)
        x_lo = pipe // (2 * depth_pipe)

        def depth_peer(step):
            return ((x_lo * depth_pipe + lax.rem(z + step, depth_pipe)) * 2 + core, ctx)

        def quad_peer(step):
            there = lax.rem(x_lo * 2 + core + step, 4)
            return (((there // 2) * depth_pipe + z) * 2 + lax.rem(there, 2), ctx)

    else:

        def depth_peer(step):
            return (pipe, ctx)

        def quad_peer(step):
            return (lax.rem(pipe + step, lanes_pipe), ctx)

    def ctx_peer(step):
        return (pipe, lax.rem(ctx + step, CTX))

    after = (lax.rem(pipe + 1, pipe_count), ctx)
    before = (lax.rem(pipe + pipe_count - 1, pipe_count), ctx)
    per_half = pipe_count // 2
    place = lax.rem(pipe, per_half)
    half_after = (pipe - place + lax.rem(place + 1, per_half), ctx)
    half_before = (pipe - place + lax.rem(place + per_half - 1, per_half), ctx)
    inner, edge, relaying = place < per_half - 1, pipe == per_half - 1, pipe == pipe_count - 1

    def own_rows(m):
        return gathered.at[m, pl.ds(pl.multiple_of(ctx * rows, rows), rows)]

    loads = [pltpu.make_async_copy(inflow.at[0, m], own_rows(m), load_sems.at[m]) for m in range(clips)]
    share = mod_weight.shape[0]
    time_cols = w_time.shape[1]
    shares = time_cols // share
    rank = pipe * CTX + ctx
    time_load = pltpu.make_async_copy(
        time_weight.at[:, pl.ds(pl.multiple_of((rank // shares) * time_cols, 128), time_cols)],
        w_time,
        load_sems.at[clips],
    )
    layer_load = pltpu.make_async_copy(layer_table, w_layer, load_sems.at[clips + 1])
    patch_loads = [
        pltpu.make_async_copy(patch_weight, w_patch, load_sems.at[clips + 2]),
        pltpu.make_async_copy(patches, patch_rows, load_sems.at[clips + 3]),
    ]
    weights = [
        pltpu.make_async_copy(w.at[0], w_all.at[:, pl.ds(i * local_cols, local_cols)], load_sems.at[clips + 4 + i])
        for i, w in enumerate((q_weight, k_weight, v_weight))
    ] + [pltpu.make_async_copy(out_weight.at[0], w_out, load_sems.at[clips + 7])]

    @pl.when(pipe > 0)
    def _():
        for copy in loads:
            copy.start()

    @pl.when(pipe == 0)
    def _():
        for copy in patch_loads:
            copy.start()

    time_load.start()
    layer_load.start()

    greeted = (
        [ctx_peer(s) for s in range(1, CTX)]
        + [depth_peer(s) for s in range(1, depth_pipe)]
        + [quad_peer(s) for s in range(1, lanes_pipe)]
        + [after, before, half_after, half_before]
    )
    barrier = pltpu.get_barrier_semaphore()
    for peer in greeted:
        pl.semaphore_signal(barrier, inc=1, device_id=peer, device_id_type=MESH)

    lane = lax.broadcasted_iota(jnp.int32, (8, rates.shape[1]), 1)
    line = lax.broadcasted_iota(jnp.int32, (8, rates.shape[1]), 0)
    steps = jnp.where(line == 0, timesteps[0], timesteps[1]).astype(jnp.float32)
    angles = steps * rates[0:1, :]
    features = jnp.where(lane < rates.shape[1] // 2, jnp.cos(angles), jnp.sin(angles)).astype(jnp.bfloat16)
    time_load.wait()
    time_hidden = jax.nn.silu(
        jnp.dot(features, w_time[...], preferred_element_type=jnp.float32)
    ).astype(jnp.bfloat16)
    first = lax.rem(rank, shares) * share
    picked = lax.broadcasted_iota(jnp.int32, (time_cols, 128), 0) - first
    picks = (picked == lax.broadcasted_iota(jnp.int32, (time_cols, 128), 1)).astype(jnp.bfloat16)
    time_piece = jnp.dot(time_hidden, picks, preferred_element_type=jnp.float32).astype(jnp.bfloat16)
    mod_part[...] = jnp.dot(
        time_piece[:, :share], mod_weight[...], preferred_element_type=jnp.float32
    )[:clips]

    @pl.when(pipe == 0)
    def _():
        for copy in patch_loads:
            copy.wait()
        for m in range(clips):
            embedded = jnp.dot(patch_rows[m], w_patch[...], preferred_element_type=jnp.float32)
            gathered[m, pl.ds(pl.multiple_of(ctx * rows, rows), rows)] = embedded.astype(jnp.bfloat16)

    @pl.when(pipe > 0)
    def _():
        for copy in loads:
            copy.wait()

    pl.semaphore_wait(barrier, len(greeted))

    def remote(src, dst, number, peer, sends=send_sems, recvs=recv_sems):
        return pltpu.make_async_remote_copy(
            src_ref=src,
            dst_ref=dst,
            send_sem=sends.at[number],
            recv_sem=recvs.at[number],
            device_id=peer,
            device_id_type=MESH,
        )

    def block(ref, m, owner, first=0, count=rows, cols=slice(None)):
        return ref.at[m, pl.ds(pl.multiple_of(owner * rows + first, 16), count), cols]

    half = rows // 2
    seen = set()

    def arrived(*copies):
        for copy in copies:
            if id(copy) not in seen:
                seen.add(id(copy))
                copy.wait_recv()

    class Gather:
        def __init__(self, m, part, columns_of):
            base = (m * PARTS + part) * PER_PART + GATHER
            whole, straight, crossing = columns_of

            def send(owner, number, peer, first=0, count=rows, cols=whole):
                piece = block(gathered if m == 0 else normed, m, owner, first, count, cols)
                return remote(piece, piece, base + number, peer)

            self.own = [send(ctx, 0, up), send(ctx, 1, down), send(ctx, 2, pair)]
            self.far_up = send(c_down, 3, up, 0, half)
            self.far_down = send(c_up, 4, down, half, half)
            self.other_up = send(c_pair, 5, up, cols=straight)
            self.other_down = send(c_pair, 6, down, cols=straight)
            self.far_pair = send(c_far, 7, pair)
            self.cross_up = send(c_down, 8, pair, cols=crossing)
            self.cross_down = send(c_up, 9, pair, cols=crossing)
            self.rest = [self.other_up, self.other_down, self.cross_up, self.cross_down, self.far_pair]
            self.all = self.own + [self.far_up, self.far_down] + self.rest

        def start(self):
            self.own[0].start()
            self.own[1].start()

        def start_pair(self):
            self.own[2].start()

        def near_up(self):
            arrived(self.own[0])
            self.far_up.start()
            self.cross_up.start()

        def near_down(self):
            arrived(self.own[1])
            self.far_down.start()
            self.cross_down.start()

        def near_pair(self):
            arrived(self.own[2])
            self.other_up.start()
            self.other_down.start()

        def far(self):
            arrived(self.far_up)
            arrived(self.far_down)
            self.far_pair.start()

        def finish(self):
            arrived(*self.own, self.far_up, self.far_down, *self.rest)

        def drain(self):
            for copy in self.all:
                copy.wait_send()

    gathers = [
        [Gather(m, i, columns_of) for i, columns_of in enumerate(column_parts(width, parts, 6))]
        for m, parts in enumerate(GATHER_PARTS)
    ]

    def add_into(m, owner, first, count, sources, cols):
        def step(i, carry):
            at = pl.ds(pl.multiple_of(owner * rows + first + i * CHUNK, CHUNK), CHUNK)
            total = partial[m, at, cols].astype(jnp.float32)
            for source in sources:
                total = total + source[pl.ds(i * CHUNK, CHUNK), cols].astype(jnp.float32)
            partial[m, at, cols] = total.astype(jnp.bfloat16)
            return carry

        lax.fori_loop(0, count // CHUNK, step, 0)

    class Reduce:
        def __init__(self, m, part, columns_of):
            self.m = m
            base = (m * PARTS + part) * PER_PART + REDUCE
            self.whole, self.straight, self.crossing = whole, straight, crossing = columns_of

            def send(owner, number, peer, into, first=0, count=rows, cols=whole):
                return remote(
                    block(partial, m, owner, first, count, cols), into.at[:, cols], base + number, peer
                )

            self.full = full = [got_full.at[m, i] for i in range(6)]
            self.halves = halves = [got_half.at[m, i] for i in range(2)]
            self.crossed = crossed = [got_cross.at[m, i] for i in range(2)]
            self.far_pair = send(c_pair_far, 0, pair, full[0])
            self.other_up = send(c_pair_up, 1, up, full[1], cols=straight)
            self.other_down = send(c_pair_down, 2, down, full[2], cols=straight)
            if CROSSED_REDUCE:
                self.cross_up = send(c_pair_up, 8, pair, crossed[0], cols=crossing)
                self.cross_down = send(c_pair_down, 9, pair, crossed[1], cols=crossing)
            result = block(partial, m, ctx, cols=whole)
            self.hand = remote(result, out_ref.at[m, :, whole], base + 10, after)
            self.hand_over = remote(result, relay.at[:, whole], base + 11, (pipe_count - 1, ctx))
            self.hand_on = remote(relay.at[:, whole], out_ref.at[m, :, whole], base + 10, half_after)
            self.far_down = send(c_far, 3, down, halves[0], 0, half)
            self.far_up = send(c_far, 4, up, halves[1], half, half)
            self.near_down = send(c_down, 5, down, full[3])
            self.near_up = send(c_up, 6, up, full[4])
            self.pair = send(c_pair, 7, pair, full[5])
            self.all = [
                self.far_pair,
                self.other_up,
                self.other_down,
                self.far_down,
                self.far_up,
                self.near_down,
                self.near_up,
                self.pair,
            ]
            if CROSSED_REDUCE:
                self.all += [self.cross_up, self.cross_down]

        def start(self):
            self.other_up.start()
            self.other_down.start()

        def start_far(self):
            self.far_pair.start()

        def start_cross(self):
            if CROSSED_REDUCE:
                self.cross_up.start()
                self.cross_down.start()

        def add_far(self):
            arrived(self.far_pair)
            add_into(self.m, c_far, 0, rows, [self.full[0]], self.whole)
            self.far_down.start()
            self.far_up.start()

        def add_pair(self):
            arrived(self.other_up)
            arrived(self.other_down)
            add_into(self.m, c_pair, 0, rows, self.full[1:3], self.straight)
            self.pair.start()

        def add_cross(self):
            if not CROSSED_REDUCE:
                return
            arrived(self.cross_up)
            arrived(self.cross_down)
            add_into(self.m, c_up, 0, rows, [self.crossed[0]], self.crossing)
            add_into(self.m, c_down, 0, rows, [self.crossed[1]], self.crossing)

        def add_near(self):
            arrived(self.far_down)
            add_into(self.m, c_down, 0, half, [self.halves[0]], self.whole)
            self.near_down.start()
            arrived(self.far_up)
            add_into(self.m, c_up, half, half, [self.halves[1]], self.whole)
            self.near_up.start()

        def last(self):
            arrived(self.near_down)
            arrived(self.near_up)
            arrived(self.pair)
            m = self.m
            cols = self.whole
            gate = modulation[pl.ds(m, 1), 2 * width + cols.start : 2 * width + cols.stop]

            def step(i, carry):
                at = pl.ds(pl.multiple_of(ctx * rows + i * CHUNK, CHUNK), CHUNK)
                here = pl.ds(i * CHUNK, CHUNK)
                branch = partial[m, at, cols].astype(jnp.float32)
                for source in self.full[3:]:
                    branch = branch + source[here, cols].astype(jnp.float32)
                result = gathered[m, at, cols].astype(jnp.float32) + gate * branch
                partial[m, at, cols] = result.astype(jnp.bfloat16)
                return carry

            lax.fori_loop(0, rows // CHUNK, step, 0)

            @pl.when(inner if m == 0 else pipe < pipe_count - 1)
            def _():
                self.hand.start()

            if m == 0:

                @pl.when(edge)
                def _():
                    self.hand_over.start()

        def pass_on(self):
            @pl.when(relaying)
            def _():
                self.hand_over.wait_recv()
                self.hand_on.start()

        def drain(self):
            for copy in self.all:
                copy.wait_send()

    reduces = [
        [Reduce(m, i, columns_of) for i, columns_of in enumerate(column_parts(width, parts, width))]
        for m, parts in enumerate(REDUCE_PARTS)
    ]

    def finish_modulation():
        layer_load.wait()
        ids = lax.broadcasted_iota(jnp.int32, (8, w_layer.shape[0]), 1)
        chosen = (ids == section_layer[pipe]).astype(jnp.bfloat16)
        layer = jnp.dot(chosen, w_layer[...], preferred_element_type=jnp.float32)
        modulation[...] = mod_total[...] + layer[:clips]

    def rotary_tables():
        cells = jnp.broadcast_to(token_cell[...].astype(jnp.float32), (HEAD, tokens)).T
        columns[...] = cells
        part = 64

        def step(i, carry):
            at = pl.ds(pl.multiple_of(i * part, part), part)
            cell = columns[at].astype(jnp.int32)
            entry = lax.broadcasted_iota(jnp.int32, (part, HEAD), 1)
            pair_id = entry & (HEAD // 2 - 1)
            place = jnp.where(
                pair_id < TIME_PAIRS,
                cell // (GRID_H * GRID_W),
                jnp.where(pair_id < TIME_PAIRS + SPACE_PAIRS, lax.rem(cell // GRID_W, GRID_H), lax.rem(cell, GRID_W)),
            )
            turn = place.astype(jnp.float32) * rates[1:2, :HEAD]
            cos_ref[at] = jnp.cos(turn)
            sin_ref[at] = jnp.where(entry < HEAD // 2, -1.0, 1.0) * jnp.sin(turn)
            return carry

        lax.fori_loop(0, tokens // part, step, 0)

    def norm_block(m, owner):
        shift = modulation[pl.ds(m, 1), 0:width]
        scale = 1.0 + modulation[pl.ds(m, 1), width : 2 * width]

        def step(i, carry):
            at = pl.ds(pl.multiple_of(owner * rows + i * CHUNK, CHUNK), CHUNK)
            values = gathered[m, at].astype(jnp.float32)
            center = values - jnp.mean(values, -1, keepdims=True)
            spread = jnp.mean(center * center, -1, keepdims=True)
            normed[m, at] = (center * lax.rsqrt(spread + 1e-06) * scale + shift).astype(jnp.bfloat16)
            return carry

        lax.fori_loop(0, rows // CHUNK, step, 0, unroll=True)

    def project(m):
        raw[...] = jnp.dot(normed[m], w_all[:, : 2 * local_cols], preferred_element_type=jnp.float32)

    def project_values(m):
        heads_v[...] = jnp.dot(
            normed[m], w_all[:, 2 * local_cols :], preferred_element_type=jnp.float32
        ).astype(jnp.bfloat16)

    stat_sends = [
        [
            remote(stat_own.at[m], stat_got.at[m, s - 1], clips * PARTS * PER_PART + m * STATS + s - 1, ctx_peer(s))
            for s in range(1, CTX)
        ]
        for m in range(clips)
    ]

    def start_stats(m):
        q_raw = raw[:, 0:local_cols]
        k_raw = raw[:, local_cols : 2 * local_cols]
        q_sum = jnp.sum(q_raw * q_raw, -1, keepdims=True)
        k_sum = jnp.sum(k_raw * k_raw, -1, keepdims=True)
        lane = lax.broadcasted_iota(jnp.int32, (tokens, HEAD), 1)
        both = jnp.where(lane == 0, q_sum, k_sum)
        stat_own[m] = both.T[0:2]
        for copy in stat_sends[m]:
            copy.start()

    def finish_stats(m):
        total = stat_own[m]
        for s, copy in enumerate(stat_sends[m]):
            copy.wait_recv()
            total = total + stat_got[m, s]
        inverse = lax.rsqrt(total / width + 1e-06)
        columns[...] = jnp.concatenate([inverse, jnp.zeros((HEAD - 2, tokens), jnp.float32)], 0).T

    def rope(m):
        def step(h, carry):
            for kind, (gain, target) in enumerate(((q_gain, heads_q), (k_gain, heads_k))):
                here = pl.ds(pl.multiple_of(h * HEAD, HEAD), HEAD)
                there = pl.ds(pl.multiple_of(kind * local_cols + h * HEAD, HEAD), HEAD)
                value = raw[:, there] * columns[:, kind : kind + 1] * gain[:, here]
                turned = value * cos_ref[...] + pltpu.roll(value, HEAD // 2, 1) * sin_ref[...]
                target[:, here] = turned.astype(jnp.bfloat16)
            return carry

        lax.fori_loop(0, local_heads, step, 0)

    q_rows = 256

    def attend(m, head, heads=1):
        def step(i, carry):
            h, r = i // (tokens // q_rows), lax.rem(i, tokens // q_rows)
            here = pl.ds(pl.multiple_of(h * HEAD, HEAD), HEAD)
            at = pl.ds(pl.multiple_of(r * q_rows, q_rows), q_rows)
            scores = lax.dot_general(
                heads_q[at, here], heads_k[:, here], (((1,), (1,)), ((), ())), preferred_element_type=jnp.float32
            ) * HEAD ** (-0.5)
            scores = scores - jnp.max(scores, -1, keepdims=True)
            weights = jnp.exp(scores)
            total = jnp.sum(weights, -1, keepdims=True)
            mixed = jnp.dot(weights.astype(jnp.bfloat16), heads_v[:, here], preferred_element_type=jnp.float32)
            attended[at, here] = (mixed / total).astype(jnp.bfloat16)
            return carry

        lax.fori_loop(head * (tokens // q_rows), (head + heads) * (tokens // q_rows), step, 0)

    out_cols = 512

    def project_out(m, part, parts):
        first, last = (width // out_cols // parts * i for i in (part, part + 1))

        def step(i, carry):
            cols = pl.ds(pl.multiple_of(i * out_cols, out_cols), out_cols)
            partial[m, :, cols] = jnp.dot(
                attended[...], w_out[:, cols], preferred_element_type=jnp.float32
            ).astype(jnp.bfloat16)
            return carry

        lax.fori_loop(first, last, step, 0)

    def mod_slice(ref, index):
        return ref.at[:, pl.ds(pl.multiple_of(index * mod_cols, 128), mod_cols)]

    mod_a = [
        remote(
            mod_slice(mod_part, lax.rem(ctx + s, CTX)), mod_got_a.at[s - 1], s - 1, ctx_peer(s), mod_send, mod_recv
        )
        for s in range(1, CTX)
    ]
    number = CTX - 1
    mod_b = [
        remote(mod_sum.at[1], mod_got_b.at[s - 1], number + s - 1, depth_peer(s), mod_send, mod_recv)
        for s in range(1, depth_pipe)
    ]
    number += depth_pipe - 1
    mod_c = [
        remote(mod_sum.at[0], mod_got_c.at[s - 1], number + s - 1, quad_peer(s), mod_send, mod_recv)
        for s in range(1, lanes_pipe)
    ]
    number += lanes_pipe - 1
    mod_d = [
        remote(mod_slice(mod_total, ctx), mod_slice(mod_total, ctx), number + s - 1, ctx_peer(s), mod_send, mod_recv)
        for s in range(1, CTX)
    ]
    own_cols = pl.ds(pl.multiple_of(ctx * mod_cols, 128), mod_cols)

    def summed(value, copies, got):
        for i, copy in enumerate(copies):
            copy.wait_recv()
            value = value + got[i]
        return value

    g0, g1 = gathers
    r0, r1 = reduces
    for copy in mod_a:
        copy.start()
    g0[1].start()
    g0[1].start_pair()
    g0[0].start()
    mod_sum[0] = summed(mod_part[:, own_cols], mod_a, mod_got_a)
    for copy in mod_c:
        copy.start()
    g0[0].start_pair()
    g0[1].near_down()
    mod_sum[1] = summed(mod_sum[0], mod_c, mod_got_c)
    for copy in mod_b:
        copy.start()
    g0[1].near_up()
    g0[0].near_down()
    g0[0].near_up()
    mod_total[:, own_cols] = summed(mod_sum[1], mod_b, mod_got_b)
    for copy in mod_d:
        copy.start()
    g0[1].far()
    g0[1].near_pair()
    g0[0].near_pair()
    g0[0].far()
    for copy in weights:
        copy.start()
    rotary_tables()
    for copy in mod_d:
        copy.wait_recv()
    finish_modulation()
    arrived(g0[0].own[1], g0[1].own[1])
    norm_block(0, c_up)
    norm_block(1, ctx)
    g1[1].start()
    g1[1].start_pair()
    arrived(g0[0].own[0], g0[1].own[0])
    norm_block(0, c_down)
    arrived(g0[0].own[2], g0[1].own[2])
    norm_block(0, c_pair)
    arrived(g0[0].far_up, g0[0].far_down, g0[1].far_up, g0[1].far_down)
    norm_block(0, c_far)
    g1[0].start()
    arrived(g0[0].other_up, g0[0].cross_up, g0[1].other_up, g0[1].cross_up)
    norm_block(0, c_pair_down)
    norm_block(0, ctx)
    arrived(g0[0].other_down, g0[0].cross_down, g0[1].other_down, g0[1].cross_down)
    norm_block(0, c_pair_up)
    g1[0].start_pair()
    arrived(g0[0].far_pair, g0[1].far_pair)
    norm_block(0, c_pair_far)
    for copy in weights:
        copy.wait()
    project(0)
    start_stats(0)
    g1[1].near_up()
    g1[1].near_down()
    g1[0].near_down()
    g1[0].near_up()
    g1[1].near_pair()
    project_values(0)
    g1[1].far()
    g1[0].near_pair()
    g1[0].far()
    finish_stats(0)
    rope(0)
    attend(0, 0)
    attend(0, 1)
    attend(0, 2)
    project_out(0, 0, 2)
    r0[0].start_far()
    r0[0].start()
    project_out(0, 1, 2)
    r0[1].start()
    r0[1].start_far()
    for gather in g1:
        gather.finish()
    project(1)
    start_stats(1)
    r0[0].start_cross()
    r0[1].start_cross()
    r0[0].add_far()
    r0[0].add_pair()
    project_values(1)
    r0[1].add_pair()
    r0[1].add_far()
    r0[0].add_cross()
    r0[0].add_near()
    r0[1].add_cross()
    finish_stats(1)
    rope(1)
    r0[1].add_near()
    attend(1, 0)
    attend(1, 1)
    attend(1, 2)
    project_out(1, 0, 2)
    r1[0].start_far()
    r1[0].start()
    project_out(1, 1, 2)
    r0[0].last()
    r1[1].start_far()
    r1[1].start()
    r0[1].last()
    r1[0].add_far()
    r1[0].start_cross()
    r1[1].start_cross()
    r1[1].add_far()
    r1[0].add_cross()
    r1[0].add_pair()
    r1[0].add_near()
    r1[1].add_pair()
    r1[1].add_cross()
    r1[1].add_near()
    for copy in mod_a + mod_b + mod_c + mod_d + stat_sends[0] + stat_sends[1]:
        copy.wait_send()
    for gather in g0 + g1:
        gather.drain()
    for reduce in r0:
        reduce.drain()
        reduce.pass_on()
    r1[0].last()
    r1[1].last()

    for reduce in r1:
        reduce.drain()
    @pl.when(inner)
    def _():
        for reduce in r0:
            reduce.hand.wait_send()

    @pl.when(edge)
    def _():
        for reduce in r0:
            reduce.hand_over.wait_send()

    @pl.when(relaying)
    def _():
        for reduce in r0:
            reduce.hand_on.wait_send()

    @pl.when(pipe < pipe_count - 1)
    def _():
        for reduce in r1:
            reduce.hand.wait_send()

    @pl.when(pipe > 0)
    def _():
        for reduce in r0 + r1:
            reduce.hand.wait_recv()


def shards(
    inflow,
    patches,
    patch_weight,
    timesteps,
    time_weight,
    mod_weight,
    layer_table,
    section_layer,
    token_cell,
    q_weight,
    k_weight,
    v_weight,
    out_weight,
    q_gain,
    k_gain,
):
    clips, rows, width = inflow.shape[1:]
    local_cols = q_weight.shape[2]
    tokens = rows * CTX
    pipe_count = lax.axis_size("pipe")
    smem = pl.BlockSpec(memory_space=pltpu.SMEM)
    vmem = pl.BlockSpec(memory_space=pltpu.VMEM)
    anywhere = pl.BlockSpec(memory_space=pl.ANY)
    mod_width = mod_weight.shape[1]
    freq_count = time_weight.shape[0]
    time_cols = 32 * mod_weight.shape[0]
    mod_cols = mod_width // CTX
    lanes_pipe = min(4, pipe_count)
    depth_pipe = pipe_count // lanes_pipe
    mod_copies = 2 * (CTX - 1) + depth_pipe - 1 + lanes_pipe - 1
    bf16, f32 = jnp.bfloat16, jnp.float32
    handed = pl.pallas_call(
        functools.partial(section_kernel, pipe_count),
        out_shape=jax.ShapeDtypeStruct((clips, rows, width), bf16),
        in_specs=[smem, smem] + [anywhere] * 4 + [vmem, anywhere, vmem, vmem] + [anywhere] * 4 + [vmem, vmem],
        out_specs=anywhere,
        scratch_shapes=[
            pltpu.VMEM((clips, tokens, width), bf16),
            pltpu.VMEM((clips, tokens, width), bf16),
            pltpu.VMEM((width, 3 * local_cols), bf16),
            pltpu.VMEM((local_cols, width), bf16),
            pltpu.VMEM((tokens, 2 * local_cols), f32),
            pltpu.VMEM((tokens, local_cols), bf16),
            pltpu.VMEM((tokens, local_cols), bf16),
            pltpu.VMEM((tokens, local_cols), bf16),
            pltpu.VMEM((tokens, local_cols), bf16),
            pltpu.VMEM((clips, tokens, width), bf16),
            pltpu.VMEM((clips, 6, rows, width), bf16),
            pltpu.VMEM((clips, 2, rows // 2, width), bf16),
            pltpu.VMEM((clips, 2, rows, width), bf16),
            pltpu.VMEM((clips, 2, tokens), f32),
            pltpu.VMEM((clips, CTX - 1, 2, tokens), f32),
            pltpu.VMEM((tokens, HEAD), f32),
            pltpu.VMEM((2, clips, mod_cols), f32),
            pltpu.VMEM((CTX - 1, clips, mod_cols), f32),
            pltpu.VMEM((max(depth_pipe - 1, 1), clips, mod_cols), f32),
            pltpu.VMEM((max(lanes_pipe - 1, 1), clips, mod_cols), f32),
            pltpu.VMEM((clips, mod_width), f32),
            pltpu.VMEM((clips, mod_width), f32),
            pltpu.VMEM((clips, mod_width), f32),
            pltpu.VMEM((tokens, HEAD), f32),
            pltpu.VMEM((tokens, HEAD), f32),
            pltpu.VMEM((freq_count, time_cols), bf16),
            pltpu.VMEM(patch_weight.shape, bf16),
            pltpu.VMEM(layer_table.shape, bf16),
            pltpu.VMEM(patches.shape, bf16),
            pltpu.VMEM((rows, width), bf16),
            pltpu.SemaphoreType.DMA((clips * (PARTS * PER_PART + STATS),)),
            pltpu.SemaphoreType.DMA((clips * (PARTS * PER_PART + STATS),)),
            pltpu.SemaphoreType.DMA((mod_copies,)),
            pltpu.SemaphoreType.DMA((mod_copies,)),
            pltpu.SemaphoreType.DMA((clips + 8,)),
        ],
        compiler_params=pltpu.CompilerParams(
            collective_id=0, has_side_effects=True, vmem_limit_bytes=56 * 2**20
        ),
        cost_estimate=pl.CostEstimate(
            flops=2 * clips * tokens * width * local_cols * 4, bytes_accessed=4 * width * local_cols * 2, transcendentals=0
        ),
    )(
        timesteps,
        section_layer,
        inflow,
        patches,
        patch_weight,
        time_weight,
        mod_weight,
        layer_table,
        token_cell[None],
        rate_rows(freq_count),
        q_weight,
        k_weight,
        v_weight,
        out_weight,
        q_gain,
        k_gain,
    )
    return jnp.where(lax.axis_index("pipe") == 0, 0, handed).astype(bf16)[None]


def solution(mesh):
    placed = (
        P("pipe", None, "ctx", None),
        P(None, "ctx", None),
        P(),
        P(),
        P(),
        P(("pipe", "ctx"), None),
        P(),
        P(),
        P(),
        P("pipe", None, "ctx"),
        P("pipe", None, "ctx"),
        P("pipe", None, "ctx"),
        P("pipe", "ctx", None),
        P("pipe", "ctx"),
        P("pipe", "ctx"),
    )
    return jax.shard_map(
        shards, mesh=mesh, in_specs=placed, out_specs=P("pipe", None, "ctx", None), check_vma=False
    )
```

```python
import functools

import jax
import jax.numpy as jnp
import numpy as np
from jax import lax
from jax.experimental import pallas as pl
from jax.experimental.pallas import tpu as pltpu
from jax.sharding import PartitionSpec as P

HEAD = 128
GRID_H = 8
GRID_W = 16
MESH = pl.DeviceIdType.MESH
CTX = 8
CHUNK = 16
SPACE_PAIRS = HEAD // 6
TIME_PAIRS = HEAD // 2 - 2 * SPACE_PAIRS

GATHER_PARTS = (2, 2)
REDUCE_PARTS = (2, 2)
PARTS = 2
GATHER = 0
REDUCE = 10
PER_PART = 22
CROSSED_REDUCE = False
STATS = CTX - 1


def column_parts(width, parts, cross_share):
    span = width // parts
    cross = span // cross_share // 128 * 128
    return [
        (slice(p * span, (p + 1) * span), slice(p * span, (p + 1) * span - cross), slice((p + 1) * span - cross, (p + 1) * span))
        for p in range(parts)
    ]


def rate_rows(freq_count):
    half_freq = freq_count // 2
    time_rates = 10000.0 ** (-np.arange(half_freq) / half_freq)
    half_size = HEAD // 2
    pair_ids = np.arange(half_size)
    exponent = np.where(
        pair_ids < TIME_PAIRS,
        pair_ids / TIME_PAIRS,
        np.where(
            pair_ids < TIME_PAIRS + SPACE_PAIRS,
            (pair_ids - TIME_PAIRS) / SPACE_PAIRS,
            (pair_ids - TIME_PAIRS - SPACE_PAIRS) / SPACE_PAIRS,
        ),
    )
    table = np.zeros((8, max(freq_count, HEAD)), np.float32)
    table[0, :freq_count] = np.concatenate([time_rates, time_rates])
    table[1, :HEAD] = np.concatenate([10000.0 ** (-exponent)] * 2)
    return table


def section_kernel(
    pipe_count,
    timesteps,
    section_layer,
    inflow,
    patches,
    patch_weight,
    time_weight,
    mod_weight,
    layer_table,
    token_cell,
    rates,
    q_weight,
    k_weight,
    v_weight,
    out_weight,
    q_gain,
    k_gain,
    out_ref,
    gathered,
    normed,
    w_all,
    w_out,
    raw,
    heads_q,
    heads_k,
    heads_v,
    attended,
    partial,
    got_full,
    got_half,
    got_cross,
    stat_own,
    stat_got,
    columns,
    mod_sum,
    mod_got_a,
    mod_got_b,
    mod_got_c,
    mod_total,
    mod_part,
    modulation,
    cos_ref,
    sin_ref,
    w_time,
    w_patch,
    w_layer,
    patch_rows,
    relay,
    send_sems,
    recv_sems,
    mod_send,
    mod_recv,
    load_sems,
):
    clips, rows, width = inflow.shape[1:]
    local_cols = q_weight.shape[2]
    local_heads = local_cols // HEAD
    tokens = rows * CTX
    mod_cols = mod_part.shape[1] // CTX
    lanes_pipe = min(4, pipe_count)
    depth_pipe = pipe_count // lanes_pipe

    pipe = lax.axis_index("pipe")
    ctx = lax.axis_index("ctx")
    y, side = ctx // 2, ctx % 2

    def at_ctx(row, col):
        return lax.rem(row + 4, 4) * 2 + col

    c_up, c_down, c_far = at_ctx(y + 1, side), at_ctx(y - 1, side), at_ctx(y + 2, side)
    c_pair = at_ctx(y, 1 - side)
    c_pair_up, c_pair_down, c_pair_far = (
        at_ctx(y + 1, 1 - side),
        at_ctx(y - 1, 1 - side),
        at_ctx(y + 2, 1 - side),
    )
    up, down, pair = (pipe, c_up), (pipe, c_down), (pipe, c_pair)

    core = lax.rem(pipe, 2)
    if pipe_count >= 4:
        z = lax.rem(pipe // 2, depth_pipe)
        x_lo = pipe // (2 * depth_pipe)

        def depth_peer(step):
            return ((x_lo * depth_pipe + lax.rem(z + step, depth_pipe)) * 2 + core, ctx)

        def quad_peer(step):
            there = lax.rem(x_lo * 2 + core + step, 4)
            return (((there // 2) * depth_pipe + z) * 2 + lax.rem(there, 2), ctx)

    else:

        def depth_peer(step):
            return (pipe, ctx)

        def quad_peer(step):
            return (lax.rem(pipe + step, lanes_pipe), ctx)

    def ctx_peer(step):
        return (pipe, lax.rem(ctx + step, CTX))

    after = (lax.rem(pipe + 1, pipe_count), ctx)
    before = (lax.rem(pipe + pipe_count - 1, pipe_count), ctx)
    per_half = pipe_count // 2
    place = lax.rem(pipe, per_half)
    half_after = (pipe - place + lax.rem(place + 1, per_half), ctx)
    half_before = (pipe - place + lax.rem(place + per_half - 1, per_half), ctx)
    inner, edge, relaying = place < per_half - 1, pipe == per_half - 1, pipe == pipe_count - 1

    def own_rows(m):
        return gathered.at[m, pl.ds(pl.multiple_of(ctx * rows, rows), rows)]

    loads = [pltpu.make_async_copy(inflow.at[0, m], own_rows(m), load_sems.at[m]) for m in range(clips)]
    share = mod_weight.shape[0]
    time_cols = w_time.shape[1]
    shares = time_cols // share
    rank = pipe * CTX + ctx
    time_load = pltpu.make_async_copy(
        time_weight.at[:, pl.ds(pl.multiple_of((rank // shares) * time_cols, 128), time_cols)],
        w_time,
        load_sems.at[clips],
    )
    layer_load = pltpu.make_async_copy(layer_table, w_layer, load_sems.at[clips + 1])
    patch_loads = [
        pltpu.make_async_copy(patch_weight, w_patch, load_sems.at[clips + 2]),
        pltpu.make_async_copy(patches, patch_rows, load_sems.at[clips + 3]),
    ]
    weights = [
        pltpu.make_async_copy(w.at[0], w_all.at[:, pl.ds(i * local_cols, local_cols)], load_sems.at[clips + 4 + i])
        for i, w in enumerate((q_weight, k_weight, v_weight))
    ] + [pltpu.make_async_copy(out_weight.at[0], w_out, load_sems.at[clips + 7])]

    @pl.when(pipe > 0)
    def _():
        for copy in loads:
            copy.start()

    @pl.when(pipe == 0)
    def _():
        for copy in patch_loads:
            copy.start()

    time_load.start()
    layer_load.start()

    greeted = (
        [ctx_peer(s) for s in range(1, CTX)]
        + [depth_peer(s) for s in range(1, depth_pipe)]
        + [quad_peer(s) for s in range(1, lanes_pipe)]
        + [after, before, half_after, half_before]
    )
    barrier = pltpu.get_barrier_semaphore()
    for peer in greeted:
        pl.semaphore_signal(barrier, inc=1, device_id=peer, device_id_type=MESH)

    lane = lax.broadcasted_iota(jnp.int32, (8, rates.shape[1]), 1)
    line = lax.broadcasted_iota(jnp.int32, (8, rates.shape[1]), 0)
    steps = jnp.where(line == 0, timesteps[0], timesteps[1]).astype(jnp.float32)
    angles = steps * rates[0:1, :]
    features = jnp.where(lane < rates.shape[1] // 2, jnp.cos(angles), jnp.sin(angles)).astype(jnp.bfloat16)
    time_load.wait()
    time_hidden = jax.nn.silu(
        jnp.dot(features, w_time[...], preferred_element_type=jnp.float32)
    ).astype(jnp.bfloat16)
    first = lax.rem(rank, shares) * share
    picked = lax.broadcasted_iota(jnp.int32, (time_cols, 128), 0) - first
    picks = (picked == lax.broadcasted_iota(jnp.int32, (time_cols, 128), 1)).astype(jnp.bfloat16)
    time_piece = jnp.dot(time_hidden, picks, preferred_element_type=jnp.float32).astype(jnp.bfloat16)
    mod_part[...] = jnp.dot(
        time_piece[:, :share], mod_weight[...], preferred_element_type=jnp.float32
    )[:clips]

    @pl.when(pipe == 0)
    def _():
        for copy in patch_loads:
            copy.wait()
        for m in range(clips):
            embedded = jnp.dot(patch_rows[m], w_patch[...], preferred_element_type=jnp.float32)
            gathered[m, pl.ds(pl.multiple_of(ctx * rows, rows), rows)] = embedded.astype(jnp.bfloat16)

    @pl.when(pipe > 0)
    def _():
        for copy in loads:
            copy.wait()

    pl.semaphore_wait(barrier, len(greeted))

    def remote(src, dst, number, peer, sends=send_sems, recvs=recv_sems):
        return pltpu.make_async_remote_copy(
            src_ref=src,
            dst_ref=dst,
            send_sem=sends.at[number],
            recv_sem=recvs.at[number],
            device_id=peer,
            device_id_type=MESH,
        )

    def block(ref, m, owner, first=0, count=rows, cols=slice(None)):
        return ref.at[m, pl.ds(pl.multiple_of(owner * rows + first, 16), count), cols]

    half = rows // 2
    seen = set()

    def arrived(*copies):
        for copy in copies:
            if id(copy) not in seen:
                seen.add(id(copy))
                copy.wait_recv()

    class Gather:
        def __init__(self, m, part, columns_of):
            base = (m * PARTS + part) * PER_PART + GATHER
            whole, straight, crossing = columns_of

            def send(owner, number, peer, first=0, count=rows, cols=whole):
                piece = block(gathered if m == 0 else normed, m, owner, first, count, cols)
                return remote(piece, piece, base + number, peer)

            self.own = [send(ctx, 0, up), send(ctx, 1, down), send(ctx, 2, pair)]
            self.far_up = send(c_down, 3, up, 0, half)
            self.far_down = send(c_up, 4, down, half, half)
            self.other_up = send(c_pair, 5, up, cols=straight)
            self.other_down = send(c_pair, 6, down, cols=straight)
            self.far_pair = send(c_far, 7, pair)
            self.cross_up = send(c_down, 8, pair, cols=crossing)
            self.cross_down = send(c_up, 9, pair, cols=crossing)
            self.rest = [self.other_up, self.other_down, self.cross_up, self.cross_down, self.far_pair]
            self.all = self.own + [self.far_up, self.far_down] + self.rest

        def start(self):
            self.own[0].start()
            self.own[1].start()

        def start_pair(self):
            self.own[2].start()

        def near_up(self):
            arrived(self.own[0])
            self.far_up.start()
            self.cross_up.start()

        def near_down(self):
            arrived(self.own[1])
            self.far_down.start()
            self.cross_down.start()

        def near_pair(self):
            arrived(self.own[2])
            self.other_up.start()
            self.other_down.start()

        def far(self):
            arrived(self.far_up)
            arrived(self.far_down)
            self.far_pair.start()

        def finish(self):
            arrived(*self.own, self.far_up, self.far_down, *self.rest)

        def drain(self):
            for copy in self.all:
                copy.wait_send()

    gathers = [
        [Gather(m, i, columns_of) for i, columns_of in enumerate(column_parts(width, parts, 12))]
        for m, parts in enumerate(GATHER_PARTS)
    ]

    def add_into(m, owner, first, count, sources, cols):
        def step(i, carry):
            at = pl.ds(pl.multiple_of(owner * rows + first + i * CHUNK, CHUNK), CHUNK)
            total = partial[m, at, cols].astype(jnp.float32)
            for source in sources:
                total = total + source[pl.ds(i * CHUNK, CHUNK), cols].astype(jnp.float32)
            partial[m, at, cols] = total.astype(jnp.bfloat16)
            return carry

        lax.fori_loop(0, count // CHUNK, step, 0)

    class Reduce:
        def __init__(self, m, part, columns_of):
            self.m = m
            base = (m * PARTS + part) * PER_PART + REDUCE
            self.whole, self.straight, self.crossing = whole, straight, crossing = columns_of

            def send(owner, number, peer, into, first=0, count=rows, cols=whole):
                return remote(
                    block(partial, m, owner, first, count, cols), into.at[:, cols], base + number, peer
                )

            self.full = full = [got_full.at[m, i] for i in range(6)]
            self.halves = halves = [got_half.at[m, i] for i in range(2)]
            self.crossed = crossed = [got_cross.at[m, i] for i in range(2)]
            self.far_pair = send(c_pair_far, 0, pair, full[0])
            self.other_up = send(c_pair_up, 1, up, full[1], cols=straight)
            self.other_down = send(c_pair_down, 2, down, full[2], cols=straight)
            if CROSSED_REDUCE:
                self.cross_up = send(c_pair_up, 8, pair, crossed[0], cols=crossing)
                self.cross_down = send(c_pair_down, 9, pair, crossed[1], cols=crossing)
            result = block(partial, m, ctx, cols=whole)
            self.hand = remote(result, out_ref.at[m, :, whole], base + 10, after)
            self.hand_over = remote(result, relay.at[:, whole], base + 11, (pipe_count - 1, ctx))
            self.hand_on = remote(relay.at[:, whole], out_ref.at[m, :, whole], base + 10, half_after)
            self.far_down = send(c_far, 3, down, halves[0], 0, half)
            self.far_up = send(c_far, 4, up, halves[1], half, half)
            self.near_down = send(c_down, 5, down, full[3])
            self.near_up = send(c_up, 6, up, full[4])
            self.pair = send(c_pair, 7, pair, full[5])
            self.all = [
                self.far_pair,
                self.other_up,
                self.other_down,
                self.far_down,
                self.far_up,
                self.near_down,
                self.near_up,
                self.pair,
            ]
            if CROSSED_REDUCE:
                self.all += [self.cross_up, self.cross_down]

        def start(self):
            self.other_up.start()
            self.other_down.start()

        def start_far(self):
            self.far_pair.start()

        def start_cross(self):
            if CROSSED_REDUCE:
                self.cross_up.start()
                self.cross_down.start()

        def add_far(self):
            arrived(self.far_pair)
            add_into(self.m, c_far, 0, rows, [self.full[0]], self.whole)
            self.far_down.start()
            self.far_up.start()

        def add_pair(self):
            arrived(self.other_up)
            arrived(self.other_down)
            add_into(self.m, c_pair, 0, rows, self.full[1:3], self.straight)
            self.pair.start()

        def add_cross(self):
            if not CROSSED_REDUCE:
                return
            arrived(self.cross_up)
            arrived(self.cross_down)
            add_into(self.m, c_up, 0, rows, [self.crossed[0]], self.crossing)
            add_into(self.m, c_down, 0, rows, [self.crossed[1]], self.crossing)

        def add_near(self):
            arrived(self.far_down)
            add_into(self.m, c_down, 0, half, [self.halves[0]], self.whole)
            self.near_down.start()
            arrived(self.far_up)
            add_into(self.m, c_up, half, half, [self.halves[1]], self.whole)
            self.near_up.start()

        def last(self):
            arrived(self.near_down)
            arrived(self.near_up)
            arrived(self.pair)
            m = self.m
            cols = self.whole
            gate = modulation[pl.ds(m, 1), 2 * width + cols.start : 2 * width + cols.stop]

            def step(i, carry):
                at = pl.ds(pl.multiple_of(ctx * rows + i * CHUNK, CHUNK), CHUNK)
                here = pl.ds(i * CHUNK, CHUNK)
                branch = partial[m, at, cols].astype(jnp.float32)
                for source in self.full[3:]:
                    branch = branch + source[here, cols].astype(jnp.float32)
                result = gathered[m, at, cols].astype(jnp.float32) + gate * branch
                partial[m, at, cols] = result.astype(jnp.bfloat16)
                return carry

            lax.fori_loop(0, rows // CHUNK, step, 0)

            @pl.when(inner if m == 0 else pipe < pipe_count - 1)
            def _():
                self.hand.start()

            if m == 0:

                @pl.when(edge)
                def _():
                    self.hand_over.start()

        def pass_on(self):
            @pl.when(relaying)
            def _():
                self.hand_over.wait_recv()
                self.hand_on.start()

        def drain(self):
            for copy in self.all:
                copy.wait_send()

    reduces = [
        [Reduce(m, i, columns_of) for i, columns_of in enumerate(column_parts(width, parts, width))]
        for m, parts in enumerate(REDUCE_PARTS)
    ]

    def finish_modulation():
        layer_load.wait()
        ids = lax.broadcasted_iota(jnp.int32, (8, w_layer.shape[0]), 1)
        chosen = (ids == section_layer[pipe]).astype(jnp.bfloat16)
        layer = jnp.dot(chosen, w_layer[...], preferred_element_type=jnp.float32)
        modulation[...] = mod_total[...] + layer[:clips]

    def rotary_tables():
        cells = jnp.broadcast_to(token_cell[...].astype(jnp.float32), (HEAD, tokens)).T
        columns[...] = cells
        part = 64

        def step(i, carry):
            at = pl.ds(pl.multiple_of(i * part, part), part)
            cell = columns[at].astype(jnp.int32)
            entry = lax.broadcasted_iota(jnp.int32, (part, HEAD), 1)
            pair_id = entry & (HEAD // 2 - 1)
            place = jnp.where(
                pair_id < TIME_PAIRS,
                cell // (GRID_H * GRID_W),
                jnp.where(pair_id < TIME_PAIRS + SPACE_PAIRS, lax.rem(cell // GRID_W, GRID_H), lax.rem(cell, GRID_W)),
            )
            turn = place.astype(jnp.float32) * rates[1:2, :HEAD]
            cos_ref[at] = jnp.cos(turn)
            sin_ref[at] = jnp.where(entry < HEAD // 2, -1.0, 1.0) * jnp.sin(turn)
            return carry

        lax.fori_loop(0, tokens // part, step, 0)

    def norm_block(m, owner):
        shift = modulation[pl.ds(m, 1), 0:width]
        scale = 1.0 + modulation[pl.ds(m, 1), width : 2 * width]

        def step(i, carry):
            at = pl.ds(pl.multiple_of(owner * rows + i * CHUNK, CHUNK), CHUNK)
            values = gathered[m, at].astype(jnp.float32)
            center = values - jnp.mean(values, -1, keepdims=True)
            spread = jnp.mean(center * center, -1, keepdims=True)
            normed[m, at] = (center * lax.rsqrt(spread + 1e-06) * scale + shift).astype(jnp.bfloat16)
            return carry

        lax.fori_loop(0, rows // CHUNK, step, 0, unroll=True)

    def project(m):
        raw[...] = jnp.dot(normed[m], w_all[:, : 2 * local_cols], preferred_element_type=jnp.float32)

    def project_values(m):
        heads_v[...] = jnp.dot(
            normed[m], w_all[:, 2 * local_cols :], preferred_element_type=jnp.float32
        ).astype(jnp.bfloat16)

    stat_sends = [
        [
            remote(stat_own.at[m], stat_got.at[m, s - 1], clips * PARTS * PER_PART + m * STATS + s - 1, ctx_peer(s))
            for s in range(1, CTX)
        ]
        for m in range(clips)
    ]

    def start_stats(m):
        q_raw = raw[:, 0:local_cols]
        k_raw = raw[:, local_cols : 2 * local_cols]
        q_sum = jnp.sum(q_raw * q_raw, -1, keepdims=True)
        k_sum = jnp.sum(k_raw * k_raw, -1, keepdims=True)
        lane = lax.broadcasted_iota(jnp.int32, (tokens, HEAD), 1)
        both = jnp.where(lane == 0, q_sum, k_sum)
        stat_own[m] = both.T[0:2]
        for copy in stat_sends[m]:
            copy.start()

    def finish_stats(m):
        total = stat_own[m]
        for s, copy in enumerate(stat_sends[m]):
            copy.wait_recv()
            total = total + stat_got[m, s]
        inverse = lax.rsqrt(total / width + 1e-06)
        columns[...] = jnp.concatenate([inverse, jnp.zeros((HEAD - 2, tokens), jnp.float32)], 0).T

    def rope(m):
        def step(h, carry):
            for kind, (gain, target) in enumerate(((q_gain, heads_q), (k_gain, heads_k))):
                here = pl.ds(pl.multiple_of(h * HEAD, HEAD), HEAD)
                there = pl.ds(pl.multiple_of(kind * local_cols + h * HEAD, HEAD), HEAD)
                value = raw[:, there] * columns[:, kind : kind + 1] * gain[:, here]
                turned = value * cos_ref[...] + pltpu.roll(value, HEAD // 2, 1) * sin_ref[...]
                target[:, here] = turned.astype(jnp.bfloat16)
            return carry

        lax.fori_loop(0, local_heads, step, 0)

    q_rows = 256

    def attend(m, head, heads=1):
        def step(i, carry):
            h, r = i // (tokens // q_rows), lax.rem(i, tokens // q_rows)
            here = pl.ds(pl.multiple_of(h * HEAD, HEAD), HEAD)
            at = pl.ds(pl.multiple_of(r * q_rows, q_rows), q_rows)
            scores = lax.dot_general(
                heads_q[at, here], heads_k[:, here], (((1,), (1,)), ((), ())), preferred_element_type=jnp.float32
            ) * HEAD ** (-0.5)
            scores = scores - jnp.max(scores, -1, keepdims=True)
            weights = jnp.exp(scores)
            total = jnp.sum(weights, -1, keepdims=True)
            mixed = jnp.dot(weights.astype(jnp.bfloat16), heads_v[:, here], preferred_element_type=jnp.float32)
            attended[at, here] = (mixed / total).astype(jnp.bfloat16)
            return carry

        lax.fori_loop(head * (tokens // q_rows), (head + heads) * (tokens // q_rows), step, 0)

    out_cols = 512

    def project_out(m, part, parts):
        first, last = (width // out_cols // parts * i for i in (part, part + 1))

        def step(i, carry):
            cols = pl.ds(pl.multiple_of(i * out_cols, out_cols), out_cols)
            partial[m, :, cols] = jnp.dot(
                attended[...], w_out[:, cols], preferred_element_type=jnp.float32
            ).astype(jnp.bfloat16)
            return carry

        lax.fori_loop(first, last, step, 0)

    def mod_slice(ref, index):
        return ref.at[:, pl.ds(pl.multiple_of(index * mod_cols, 128), mod_cols)]

    mod_a = [
        remote(
            mod_slice(mod_part, lax.rem(ctx + s, CTX)), mod_got_a.at[s - 1], s - 1, ctx_peer(s), mod_send, mod_recv
        )
        for s in range(1, CTX)
    ]
    number = CTX - 1
    mod_b = [
        remote(mod_sum.at[1], mod_got_b.at[s - 1], number + s - 1, depth_peer(s), mod_send, mod_recv)
        for s in range(1, depth_pipe)
    ]
    number += depth_pipe - 1
    mod_c = [
        remote(mod_sum.at[0], mod_got_c.at[s - 1], number + s - 1, quad_peer(s), mod_send, mod_recv)
        for s in range(1, lanes_pipe)
    ]
    number += lanes_pipe - 1
    mod_d = [
        remote(mod_slice(mod_total, ctx), mod_slice(mod_total, ctx), number + s - 1, ctx_peer(s), mod_send, mod_recv)
        for s in range(1, CTX)
    ]
    own_cols = pl.ds(pl.multiple_of(ctx * mod_cols, 128), mod_cols)

    def summed(value, copies, got):
        for i, copy in enumerate(copies):
            copy.wait_recv()
            value = value + got[i]
        return value

    g0, g1 = gathers
    r0, r1 = reduces
    for copy in mod_a:
        copy.start()
    g0[1].start()
    g0[1].start_pair()
    g0[0].start()
    mod_sum[0] = summed(mod_part[:, own_cols], mod_a, mod_got_a)
    for copy in mod_c:
        copy.start()
    g0[0].start_pair()
    g0[1].near_down()
    mod_sum[1] = summed(mod_sum[0], mod_c, mod_got_c)
    for copy in mod_b:
        copy.start()
    g0[1].near_up()
    g0[0].near_down()
    g0[0].near_up()
    mod_total[:, own_cols] = summed(mod_sum[1], mod_b, mod_got_b)
    for copy in mod_d:
        copy.start()
    g0[1].far()
    g0[1].near_pair()
    g0[0].near_pair()
    g0[0].far()
    for copy in weights:
        copy.start()
    rotary_tables()
    for copy in mod_d:
        copy.wait_recv()
    finish_modulation()
    arrived(g0[0].own[1], g0[1].own[1])
    norm_block(0, c_up)
    norm_block(1, ctx)
    g1[1].start()
    g1[1].start_pair()
    arrived(g0[0].own[0], g0[1].own[0])
    norm_block(0, c_down)
    arrived(g0[0].own[2], g0[1].own[2])
    norm_block(0, c_pair)
    arrived(g0[0].far_up, g0[0].far_down, g0[1].far_up, g0[1].far_down)
    norm_block(0, c_far)
    g1[0].start()
    arrived(g0[0].other_up, g0[0].cross_up, g0[1].other_up, g0[1].cross_up)
    norm_block(0, c_pair_down)
    norm_block(0, ctx)
    arrived(g0[0].other_down, g0[0].cross_down, g0[1].other_down, g0[1].cross_down)
    norm_block(0, c_pair_up)
    g1[0].start_pair()
    arrived(g0[0].far_pair, g0[1].far_pair)
    norm_block(0, c_pair_far)
    for copy in weights:
        copy.wait()
    project(0)
    start_stats(0)
    g1[1].near_up()
    g1[1].near_down()
    g1[0].near_down()
    g1[0].near_up()
    g1[1].near_pair()
    project_values(0)
    g1[1].far()
    g1[0].near_pair()
    g1[0].far()
    finish_stats(0)
    rope(0)
    attend(0, 0)
    attend(0, 1)
    attend(0, 2)
    project_out(0, 0, 2)
    r0[0].start_far()
    r0[0].start()
    project_out(0, 1, 2)
    r0[1].start()
    r0[1].start_far()
    for gather in g1:
        gather.finish()
    project(1)
    start_stats(1)
    r0[0].start_cross()
    r0[1].start_cross()
    r0[0].add_far()
    r0[0].add_pair()
    project_values(1)
    r0[1].add_pair()
    r0[1].add_far()
    r0[0].add_cross()
    r0[0].add_near()
    r0[1].add_cross()
    finish_stats(1)
    rope(1)
    r0[1].add_near()
    attend(1, 0)
    attend(1, 1)
    attend(1, 2)
    project_out(1, 0, 2)
    r1[0].start_far()
    r1[0].start()
    project_out(1, 1, 2)
    r0[0].last()
    r1[1].start_far()
    r1[1].start()
    r0[1].last()
    r1[0].add_far()
    r1[0].start_cross()
    r1[1].start_cross()
    r1[1].add_far()
    r1[0].add_cross()
    r1[0].add_pair()
    r1[0].add_near()
    r1[1].add_pair()
    r1[1].add_cross()
    r1[1].add_near()
    for copy in mod_a + mod_b + mod_c + mod_d + stat_sends[0] + stat_sends[1]:
        copy.wait_send()
    for gather in g0 + g1:
        gather.drain()
    for reduce in r0:
        reduce.drain()
        reduce.pass_on()
    r1[0].last()
    r1[1].last()

    for reduce in r1:
        reduce.drain()
    @pl.when(inner)
    def _():
        for reduce in r0:
            reduce.hand.wait_send()

    @pl.when(edge)
    def _():
        for reduce in r0:
            reduce.hand_over.wait_send()

    @pl.when(relaying)
    def _():
        for reduce in r0:
            reduce.hand_on.wait_send()

    @pl.when(pipe < pipe_count - 1)
    def _():
        for reduce in r1:
            reduce.hand.wait_send()

    @pl.when(pipe > 0)
    def _():
        for reduce in r0 + r1:
            reduce.hand.wait_recv()


def shards(
    inflow,
    patches,
    patch_weight,
    timesteps,
    time_weight,
    mod_weight,
    layer_table,
    section_layer,
    token_cell,
    q_weight,
    k_weight,
    v_weight,
    out_weight,
    q_gain,
    k_gain,
):
    clips, rows, width = inflow.shape[1:]
    local_cols = q_weight.shape[2]
    tokens = rows * CTX
    pipe_count = lax.axis_size("pipe")
    smem = pl.BlockSpec(memory_space=pltpu.SMEM)
    vmem = pl.BlockSpec(memory_space=pltpu.VMEM)
    anywhere = pl.BlockSpec(memory_space=pl.ANY)
    mod_width = mod_weight.shape[1]
    freq_count = time_weight.shape[0]
    time_cols = 32 * mod_weight.shape[0]
    mod_cols = mod_width // CTX
    lanes_pipe = min(4, pipe_count)
    depth_pipe = pipe_count // lanes_pipe
    mod_copies = 2 * (CTX - 1) + depth_pipe - 1 + lanes_pipe - 1
    bf16, f32 = jnp.bfloat16, jnp.float32
    handed = pl.pallas_call(
        functools.partial(section_kernel, pipe_count),
        out_shape=jax.ShapeDtypeStruct((clips, rows, width), bf16),
        in_specs=[smem, smem] + [anywhere] * 4 + [vmem, anywhere, vmem, vmem] + [anywhere] * 4 + [vmem, vmem],
        out_specs=anywhere,
        scratch_shapes=[
            pltpu.VMEM((clips, tokens, width), bf16),
            pltpu.VMEM((clips, tokens, width), bf16),
            pltpu.VMEM((width, 3 * local_cols), bf16),
            pltpu.VMEM((local_cols, width), bf16),
            pltpu.VMEM((tokens, 2 * local_cols), f32),
            pltpu.VMEM((tokens, local_cols), bf16),
            pltpu.VMEM((tokens, local_cols), bf16),
            pltpu.VMEM((tokens, local_cols), bf16),
            pltpu.VMEM((tokens, local_cols), bf16),
            pltpu.VMEM((clips, tokens, width), bf16),
            pltpu.VMEM((clips, 6, rows, width), bf16),
            pltpu.VMEM((clips, 2, rows // 2, width), bf16),
            pltpu.VMEM((clips, 2, rows, width), bf16),
            pltpu.VMEM((clips, 2, tokens), f32),
            pltpu.VMEM((clips, CTX - 1, 2, tokens), f32),
            pltpu.VMEM((tokens, HEAD), f32),
            pltpu.VMEM((2, clips, mod_cols), f32),
            pltpu.VMEM((CTX - 1, clips, mod_cols), f32),
            pltpu.VMEM((max(depth_pipe - 1, 1), clips, mod_cols), f32),
            pltpu.VMEM((max(lanes_pipe - 1, 1), clips, mod_cols), f32),
            pltpu.VMEM((clips, mod_width), f32),
            pltpu.VMEM((clips, mod_width), f32),
            pltpu.VMEM((clips, mod_width), f32),
            pltpu.VMEM((tokens, HEAD), f32),
            pltpu.VMEM((tokens, HEAD), f32),
            pltpu.VMEM((freq_count, time_cols), bf16),
            pltpu.VMEM(patch_weight.shape, bf16),
            pltpu.VMEM(layer_table.shape, bf16),
            pltpu.VMEM(patches.shape, bf16),
            pltpu.VMEM((rows, width), bf16),
            pltpu.SemaphoreType.DMA((clips * (PARTS * PER_PART + STATS),)),
            pltpu.SemaphoreType.DMA((clips * (PARTS * PER_PART + STATS),)),
            pltpu.SemaphoreType.DMA((mod_copies,)),
            pltpu.SemaphoreType.DMA((mod_copies,)),
            pltpu.SemaphoreType.DMA((clips + 8,)),
        ],
        compiler_params=pltpu.CompilerParams(
            collective_id=0, has_side_effects=True, vmem_limit_bytes=56 * 2**20
        ),
        cost_estimate=pl.CostEstimate(
            flops=2 * clips * tokens * width * local_cols * 4, bytes_accessed=4 * width * local_cols * 2, transcendentals=0
        ),
    )(
        timesteps,
        section_layer,
        inflow,
        patches,
        patch_weight,
        time_weight,
        mod_weight,
        layer_table,
        token_cell[None],
        rate_rows(freq_count),
        q_weight,
        k_weight,
        v_weight,
        out_weight,
        q_gain,
        k_gain,
    )
    return jnp.where(lax.axis_index("pipe") == 0, 0, handed).astype(bf16)[None]


def solution(mesh):
    placed = (
        P("pipe", None, "ctx", None),
        P(None, "ctx", None),
        P(),
        P(),
        P(),
        P(("pipe", "ctx"), None),
        P(),
        P(),
        P(),
        P("pipe", None, "ctx"),
        P("pipe", None, "ctx"),
        P("pipe", None, "ctx"),
        P("pipe", "ctx", None),
        P("pipe", "ctx"),
        P("pipe", "ctx"),
    )
    return jax.shard_map(
        shards, mesh=mesh, in_specs=placed, out_specs=P("pipe", None, "ctx", None), check_vma=False
    )
```
